256 devices in a mesh: leaf: 256 (over x, y, z, core).
Axes of the slice: x: 4, y: 4, z: 8, core: 2. Of those that a mesh axis runs over, the one named last changes fastest.
Arguments:
- right_sides: bfloat16 [16, 524288], P(None, 'leaf'), may hold values from -6 to 6
- point_order: int32 [256, 2048], P('leaf'), may hold values from 0 to 2047, each once within a row
- leaf_inverse: bfloat16 [524288, 2048], P('leaf')
- test_bases: bfloat16 [8, 64, 524288], P(None, None, 'leaf')
- trial_bases: bfloat16 [8, 64, 524288], P(None, None, 'leaf'), may hold values from -0.75 to 0.75
- coupling_cores: bfloat16 [8, 16384, 128], P(None, 'leaf'), as said below
Outputs:
- solution: float32 [16, 524288], P(None, 'leaf')
The draws below stay inside these ranges and needn't reach their ends.
Inputs may be any that keep to these rules, and one draw needn't show every extreme that they name: `point_order`: each row is a permutation of 0 to 2047. `coupling_cores`: at each level k, the blocks held by the leaves of one half of a node (equal d >> k) are equal.
All inputs are finite; a program needn't handle non-finite values.
Results may differ from the reference program's by a relative error of at most 0.01.
Values sent between devices are 32-bit elements; how exact they have to be, the bound alone decides.
No kernel may reach another device: no remote copies, remote signals or barrier semaphores. Data moves between devices by JAX's collectives and lax.ppermute only.
A program may use at most 64 MiB of HBM per device.

```python
import math
import jax
import jax.numpy as jnp
from jax import lax

LEAF = 2048
R = 64
RHS = 16
LEAVES = 256
LEVELS = 8
NPTS = 524288
N_LEAF = 256


def draw_leaf_inverse(key, part):
    key = jax.random.fold_in(key, 11)
    first, second = jax.random.split(key)
    spread = jax.random.normal(first, (LEAVES, LEAF, LEAF), jnp.float32)
    diag_values = jax.random.uniform(second, (LEAVES, LEAF, 1), jnp.float32, 0.5, 1.5)
    rows = lax.broadcasted_iota(jnp.int32, (LEAF, LEAF), 0)
    columns = lax.broadcasted_iota(jnp.int32, (LEAF, LEAF), 1)
    identity = (rows == columns).astype(jnp.float32)
    whole = spread * (0.5 / math.sqrt(LEAF)) + identity[None] * diag_values
    return whole.reshape(LEAVES * LEAF, LEAF).astype(jnp.bfloat16)


def draw_test_bases(key, part):
    key = jax.random.fold_in(key, 12)
    values = jax.random.normal(key, (LEVELS, R, NPTS), jnp.float32)
    level_index = lax.broadcasted_iota(jnp.int32, (LEVELS, 1, 1), 0).astype(jnp.float32)
    scale = jnp.exp2(-0.5 * level_index) / math.sqrt(LEAF)
    return (values * scale).astype(jnp.bfloat16)


def draw_coupling_cores(key, part):
    key = jax.random.fold_in(key, 13)
    values = jax.random.normal(key, (LEVELS, LEAVES, R, 2 * R), jnp.float32)
    values = values / math.sqrt(8 * R)
    leaf_index = lax.broadcasted_iota(jnp.int32, (LEVELS, LEAVES), 1)
    level_index = lax.broadcasted_iota(jnp.int32, (LEVELS, LEAVES), 0)
    half_index = jnp.right_shift(leaf_index, level_index)
    chosen = jnp.take_along_axis(values, half_index[:, :, None, None], axis=1)
    return chosen.reshape(LEVELS, LEAVES * R, 2 * R).astype(jnp.bfloat16)


def levels(key, shape, pieces, smallest, largest):
    def one(dim, shards_of):
        steps = jax.random.uniform(jax.random.fold_in(jax.random.fold_in(key, 6), dim), (shards_of,), jnp.float32, smallest / len(pieces), largest / len(pieces))
        return jnp.repeat(jnp.exp(steps), shape[dim] // shards_of).reshape((-1,) + (1,) * (len(shape) - dim - 1))

    factor_of = one(*pieces[0])
    for cut in pieces[1:]:
        factor_of = factor_of * one(*cut)
    return factor_of


def gaussian(rng, shape, deviation, limit, cuts=(), held_as=jnp.bfloat16):
    entries = deviation * jax.random.normal(rng, shape, jnp.float32)
    if cuts:
        entries = entries * levels(rng, shape, cuts, -0.22, 0.18)
    return jnp.clip(entries, -limit, limit).astype(held_as)


def setup_inputs(seed: int = 0) -> dict:
    keys = jax.random.split(jax.random.key(seed), 7)
    return {
        "right_sides": gaussian(keys[0], (RHS, NPTS), 1.0, 6.0, ((1, 256),)),
        "point_order": jax.vmap(lambda own: jax.random.permutation(own, LEAF))(jax.random.split(keys[1], LEAVES)).reshape((LEAVES, LEAF)).astype(jnp.int32),
        "leaf_inverse": draw_leaf_inverse(jax.random.fold_in(keys[6], 71), 0),
        "test_bases": draw_test_bases(jax.random.fold_in(keys[6], 71), 0),
        "trial_bases": gaussian(keys[4], (LEVELS, R, NPTS), R ** -0.5, 0.75, ((2, 256),)),
        "coupling_cores": draw_coupling_cores(jax.random.fold_in(keys[6], 71), 0),
    }


def leaf_product(pair):
    return jnp.dot(pair[0], pair[1], preferred_element_type=jnp.float32)


def place_back(positions, values):
    return jnp.zeros_like(values).at[:, positions].set(values)


def reference(right_sides, point_order, leaf_inverse, test_bases, trial_bases, coupling_cores):
    highest = lax.Precision.HIGHEST
    blocks = right_sides.reshape(RHS, N_LEAF, LEAF).transpose(1, 0, 2)
    ordered = jnp.take_along_axis(blocks, point_order[:, None, :].astype(jnp.int32), axis=2)
    inverses = leaf_inverse.reshape(N_LEAF, LEAF, LEAF)
    current = lax.map(leaf_product, (ordered, inverses))
    for level in range(LEVELS):
        rounded = current.astype(jnp.bfloat16).astype(jnp.float32)
        row_basis = test_bases[level].reshape(R, N_LEAF, LEAF).astype(jnp.float32)
        projection = jnp.einsum('dql,rdl->dqr', rounded, row_basis, precision=highest)
        halves = projection.reshape(N_LEAF >> level, 2 ** level, RHS, R).sum(axis=1)
        stacked = halves.reshape(N_LEAF >> (level + 1), 2, RHS, R).transpose(0, 2, 1, 3)
        stacked = stacked.reshape(N_LEAF >> (level + 1), RHS, 2 * R)
        stacked = jnp.repeat(stacked, 2 ** (level + 1), axis=0)
        cores = coupling_cores[level].reshape(N_LEAF, R, 2 * R).astype(jnp.float32)
        weights = jnp.einsum('dqc,drc->dqr', stacked, cores, precision=highest)
        weights = weights.astype(jnp.bfloat16).astype(jnp.float32)
        column_basis = trial_bases[level].reshape(R, N_LEAF, LEAF).astype(jnp.float32)
        current = current - jnp.einsum('dqr,rdl->dql', weights, column_basis, precision=highest)
    placed = jax.vmap(place_back)(point_order.astype(jnp.int32), current)
    return placed.transpose(1, 0, 2).reshape(RHS, N_LEAF * LEAF)
```

```python
import functools

import jax
import jax.numpy as jnp
from jax import lax
from jax.experimental import pallas as pl
from jax.experimental.pallas import tpu as pltpu
from jax.sharding import PartitionSpec as P


F32 = jnp.float32
BF16 = jnp.bfloat16
STAGES = 4
RHS = 16
RANK = 64
LANES = 128
BLOCK = 256
NT = (((1,), (1,)), ((), ()))


def mm(a, b):
    return lax.dot_general(
        a, b, (((1,), (0,)), ((), ())), precision=lax.Precision.HIGHEST, preferred_element_type=F32
    )


def mm_nt(a, b):
    return lax.dot_general(a, b, NT, precision=lax.Precision.HIGHEST, preferred_element_type=F32)


def round16(x):
    return x.astype(BF16).astype(F32)


def groups(bits, devices):
    size = 2 ** len(bits)
    out = []
    for base in range(devices):
        if any(base >> b & 1 for b in bits):
            continue
        out.append([base + sum((j >> t & 1) << b for t, b in enumerate(bits)) for j in range(size)])
    return out


def one_hot_low(positions, leaf):
    rows = lax.broadcasted_iota(jnp.int32, (LANES, leaf), 0)
    return jnp.where(rows == (positions & (LANES - 1)), 1.0, 0.0).astype(BF16)


def front_kernel(rs_ref, pos_ref, inv_ref, u_ref, v_ref, core_ref, cur_ref, pay_ref, rest_ref, ordered, proj, gram):
    step = pl.program_id(0)
    leaf = rs_ref.shape[1]
    tiles = leaf // LANES

    @pl.when(step == 0)
    def _():
        positions = pos_ref[...]
        hot = one_hot_low(positions, leaf)
        high = positions // LANES
        rows = jnp.concatenate([rs_ref[:, h * LANES : (h + 1) * LANES] for h in range(tiles)], axis=0)
        picked = jnp.dot(rows, hot, preferred_element_type=F32)
        total = jnp.zeros((RHS, leaf), F32)
        for h in range(tiles):
            total = total + jnp.where(high == h, picked[h * RHS : (h + 1) * RHS], 0.0)
        ordered[...] = total.astype(BF16)
        proj[...] = jnp.zeros_like(proj)
        gram[...] = jnp.zeros_like(gram)

    current = jnp.dot(ordered[...], inv_ref[...], preferred_element_type=F32)
    cur_ref[...] = current
    proj[...] += lax.dot_general(current.astype(BF16), u_ref[...], NT, preferred_element_type=F32)
    for a in range(STAGES):
        lo = a * LANES
        gram[lo : lo + LANES, lo:] += lax.dot_general(
            v_ref[lo : lo + LANES, :], u_ref[lo:, :], NT, preferred_element_type=F32
        )

    @pl.when(step == pl.num_programs(0) - 1)
    def _():
        lane = lax.broadcasted_iota(jnp.int32, (RANK, LANES), 1)

        def diagonal(a):
            lo = a * LANES
            return jnp.where(lane < RANK, 0.0, gram[lo : lo + RANK, lo : lo + LANES])

        pay_ref[:RHS] = proj[:, :LANES]
        pay_ref[RHS : RHS + RANK] = core_ref[0].astype(F32)
        pay_ref[RHS + RANK :] = diagonal(0)
        at = 0
        for b in range(1, STAGES):
            rest_ref[at : at + RHS] = proj[:, b * LANES : (b + 1) * LANES]
            at += RHS
        for b in range(1, STAGES):
            rest_ref[at : at + RANK] = diagonal(b)
            at += RANK
        for b in range(STAGES):
            for c in range(b + 1, STAGES):
                rest_ref[at : at + LANES] = gram[b * LANES : (b + 1) * LANES, c * LANES : (c + 1) * LANES]
                at += LANES


def tiles_after(a):
    later = STAGES - 1 - a
    return RHS * later, RANK * later, LANES * (later * (later - 1) // 2)


def solve_kernel(a, copies, got_ref, rest_ref, core_ref, w_ref, *out):
    lane = lax.broadcasted_iota(jnp.int32, (RHS, LANES), 1)
    own = lax.axis_index("leaf") >> (2 * a) & 3
    pair = [got_ref[n, :RHS] for n in range(4)]
    weights = []
    for n in range(4):
        m = n & 2
        stacked = jnp.where(lane < RANK, pair[m], pltpu.roll(pair[m + 1], RANK, 1))
        weights.append(round16(mm_nt(stacked, got_ref[n, RHS : RHS + RANK])))
    after = [pair[n] - mm(weights[n], got_ref[n, RHS + RANK :]) for n in range(4)]
    stacked = jnp.where(lane < RANK, pltpu.roll(after[0] + after[1], RANK, 1), after[2] + after[3])
    second = round16(mm_nt(stacked, core_ref[0].astype(F32)))
    first = jnp.zeros_like(second)
    for n in range(4):
        first = jnp.where(own == n, weights[n], first)
    w_ref[:, :RANK] = first
    w_ref[:, RANK:] = second
    later = STAGES - 1 - a
    if later:
        (out_ref,) = out
        n_proj, n_own, n_cross = tiles_after(a)
        cross = n_proj + n_own
        for i in range(later):
            tile = cross + i * LANES
            value = rest_ref[i * RHS : (i + 1) * RHS]
            value = value - mm(first, rest_ref[tile : tile + RANK]) - mm(second, rest_ref[tile + RANK : tile + LANES])
            for n in range(copies):
                out_ref[n, i * RHS : (i + 1) * RHS] = value
        for n in range(copies):
            out_ref[n, n_proj:cross] = rest_ref[n_proj:cross]
            if n_cross:
                out_ref[n, cross:] = rest_ref[cross + later * LANES :]


def sum_kernel(a, copies, got_ref, core_ref, pay_ref, *out):
    n_proj, n_own, n_cross = tiles_after(a - 1)

    def total(lo, hi):
        return (got_ref[0, lo:hi] + got_ref[1, lo:hi]) + (got_ref[2, lo:hi] + got_ref[3, lo:hi])

    pair = total(0, RHS)
    core = core_ref[0].astype(F32)
    diagonal = total(n_proj, n_proj + RANK)
    for n in range(copies):
        pay_ref[n, :RHS] = pair
        pay_ref[n, RHS : RHS + RANK] = core
        pay_ref[n, RHS + RANK :] = diagonal
    if out:
        (rest_ref,) = out
        m_proj, m_own, _ = tiles_after(a)
        rest_ref[:m_proj] = total(RHS, n_proj)
        rest_ref[m_proj : m_proj + m_own] = total(n_proj + RANK, n_proj + n_own)
        if n_cross:
            rest_ref[m_proj + m_own :] = total(n_proj + n_own, n_proj + n_own + n_cross)


def final_kernel(cur_ref, w0_ref, w1_ref, w2_ref, w3_ref, v_ref, pos_ref, out_ref):
    leaf = cur_ref.shape[1]
    current = cur_ref[...]
    for a, w_ref in enumerate((w0_ref, w1_ref, w2_ref, w3_ref)):
        current = current - jnp.dot(
            w_ref[...].astype(BF16), v_ref[a * LANES : (a + 1) * LANES], preferred_element_type=F32
        )
    positions = pos_ref[...]
    hot = one_hot_low(positions, leaf)
    high = positions // LANES
    first = round16(current)
    left = current - first
    second = round16(left)
    parts = jnp.concatenate([first, second, left - second], axis=0)
    for h in range(leaf // LANES):
        chosen = jnp.where(high == h, parts, 0.0).astype(BF16)
        moved = lax.dot_general(chosen, hot, NT, preferred_element_type=F32)
        out_ref[:, h * LANES : (h + 1) * LANES] = (moved[:RHS] + moved[RHS : 2 * RHS]) + moved[2 * RHS :]


def local(right_sides, point_order, leaf_inverse, test_bases, trial_bases, coupling_cores):
    devices = lax.axis_size("leaf")
    leaf = right_sides.shape[1]
    total = STAGES * LANES
    test = test_bases.reshape(total, leaf)
    trial = trial_bases.reshape(total, leaf)
    vmem = pl.BlockSpec(memory_space=pltpu.VMEM)
    params = pltpu.CompilerParams(vmem_limit_bytes=40 * 2**20)

    def core_spec(level):
        return pl.BlockSpec((1, RANK, LANES), lambda *_: (level, 0, 0))

    def shape(*dims):
        return jax.ShapeDtypeStruct(dims, F32)

    pay_rows = RHS + 2 * RANK
    rest_rows = sum(tiles_after(0)) + LANES * (STAGES - 1)
    current, pay, rest = pl.pallas_call(
        front_kernel,
        grid=(leaf // BLOCK,),
        in_specs=[
            pl.BlockSpec((RHS, leaf), lambda j: (0, 0)),
            pl.BlockSpec((1, leaf), lambda j: (0, 0)),
            pl.BlockSpec((leaf, BLOCK), lambda j: (0, j)),
            pl.BlockSpec((total, BLOCK), lambda j: (0, j)),
            pl.BlockSpec((total, BLOCK), lambda j: (0, j)),
            core_spec(0),
        ],
        out_specs=[
            pl.BlockSpec((RHS, BLOCK), lambda j: (0, j)),
            pl.BlockSpec((pay_rows, LANES), lambda j: (0, 0)),
            pl.BlockSpec((rest_rows, LANES), lambda j: (0, 0)),
        ],
        out_shape=[shape(RHS, leaf), shape(pay_rows, LANES), shape(rest_rows, LANES)],
        scratch_shapes=[
            pltpu.VMEM((RHS, leaf), BF16),
            pltpu.VMEM((RHS, total), F32),
            pltpu.VMEM((total, total), F32),
        ],
        compiler_params=params,
        name="front",
    )(right_sides, point_order, leaf_inverse, test, trial, coupling_cores)

    def exchange(values, a):
        near = groups((2 * a, 2 * a + 1), devices)
        if a == 0:
            return lax.all_gather(values, "leaf", axis=0, axis_index_groups=near, tiled=True)
        return lax.all_to_all(values, "leaf", 0, 0, axis_index_groups=near, tiled=True)

    def copies(a):
        return 1 if a == 0 else 4

    weights = []
    pay = pay[None]
    for a in range(STAGES):
        got = exchange(pay, a)
        later = STAGES - 1 - a
        out_shape = [shape(RHS, LANES)]
        if later:
            out_shape.append(shape(copies(a), sum(tiles_after(a)), LANES))
        else:
            rest = jnp.zeros((8, LANES), F32)
        solved = pl.pallas_call(
            functools.partial(solve_kernel, a, copies(a)),
            grid=(1,),
            in_specs=[vmem, vmem, core_spec(2 * a + 1)],
            out_specs=[vmem] * len(out_shape),
            out_shape=out_shape,
            compiler_params=params,
            name="solve" + str(a),
        )(got, rest, coupling_cores)
        weights.append(solved[0])
        if not later:
            break
        got = exchange(solved[1], a)
        out_shape = [shape(copies(a + 1), pay_rows, LANES)]
        if later > 1:
            out_shape.append(shape(sum(tiles_after(a + 1)) + LANES * (later - 1), LANES))
        summed = pl.pallas_call(
            functools.partial(sum_kernel, a + 1, copies(a + 1)),
            grid=(1,),
            in_specs=[vmem, core_spec(2 * a + 2)],
            out_specs=[vmem] * len(out_shape),
            out_shape=out_shape,
            compiler_params=params,
            name="sum" + str(a),
        )(got, coupling_cores)
        pay = summed[0]
        if later > 1:
            rest = summed[1]

    return pl.pallas_call(
        final_kernel,
        in_specs=[vmem] * 7,
        out_specs=vmem,
        out_shape=shape(RHS, leaf),
        compiler_params=params,
        name="last",
    )(current, *weights, trial, point_order)


def solution(mesh):
    in_specs = (
        P(None, "leaf"),
        P("leaf", None),
        P("leaf", None),
        P(None, None, "leaf"),
        P(None, None, "leaf"),
        P(None, "leaf", None),
    )
    out_specs = P(None, "leaf")
    return jax.shard_map(local, mesh=mesh, in_specs=in_specs, out_specs=out_specs, check_vma=False)
```

```python
import functools

import jax
import jax.numpy as jnp
from jax import lax
from jax.experimental import pallas as pl
from jax.experimental.pallas import tpu as pltpu
from jax.sharding import PartitionSpec as P


F32 = jnp.float32
BF16 = jnp.bfloat16
PAIRS = 4
RHS = 16
RANK = 64
LANES = 128
WIDE = 256
CHUNKS = 4
NT = (((1,), (1,)), ((), ()))
MESSAGE = RHS + 2 * RANK


def split(x, parts):
    out = []
    for _ in range(parts):
        piece = x.astype(BF16)
        out.append(piece)
        x = x - piece.astype(F32)
    return out


def times(weights, product):
    high, low = split(product, 2)
    return jnp.dot(weights, high, preferred_element_type=F32) + jnp.dot(weights, low, preferred_element_type=F32)


def core_times(stacked, cores):
    rows = stacked.shape[0]
    out = lax.dot_general(jnp.concatenate(split(stacked, 3), axis=0), cores, NT, preferred_element_type=F32)
    return (out[:rows] + (out[rows : 2 * rows] + out[2 * rows :])).astype(BF16)


def lanes(rows=RHS):
    return lax.broadcasted_iota(jnp.int32, (rows, LANES), 1)


def swap(x):
    return pltpu.roll(x, RANK, 1)


def bit(k):
    return lax.axis_index("leaf") >> k & 1


def order(k, own, far):
    upper = bit(k) == 1
    return jnp.where(upper, far, own), jnp.where(upper, own, far)


def side_by_side(k, low, high):
    if k % 2:
        return jnp.where(lanes() < RANK, swap(low), high)
    return jnp.where(lanes() < RANK, low, swap(high))


def one_hot_low(positions, leaf):
    rows = lax.broadcasted_iota(jnp.int32, (WIDE, leaf), 0)
    return jnp.where(rows == (positions & (WIDE - 1)), 1.0, 0.0).astype(BF16)


def gather_points(sides, positions):
    leaf = sides.shape[1]
    sides = sides.astype(BF16)
    positions = positions.astype(jnp.int32)
    high = positions // WIDE
    rows = jnp.concatenate([sides[:, h * WIDE : (h + 1) * WIDE] for h in range(leaf // WIDE)], axis=0)
    picked = jnp.dot(rows, one_hot_low(positions, leaf), preferred_element_type=F32)
    total = jnp.zeros((RHS, leaf), F32)
    for h in range(leaf // WIDE):
        total = total + jnp.where(high == h, picked[h * RHS : (h + 1) * RHS], 0.0)
    return total.astype(BF16)


def front_kernel(
    rows_ref, inv_hbm, u_hbm, v_hbm, cur_ref, pay_ref, rest_ref, near_ref, keep_ref, send_ref,
    inv, u, v, ordered, proj, gram, sems,
):
    leaf = rows_ref.shape[1]
    width = leaf // CHUNKS
    copies = []
    for j in range(CHUNKS):
        at = pl.ds(j * width, width)
        copies.append(
            [
                pltpu.make_async_copy(inv_hbm.at[:, at], inv.at[:, at], sems.at[0, j]),
                pltpu.make_async_copy(u_hbm.at[:, at], u.at[:, at], sems.at[1, j]),
                pltpu.make_async_copy(v_hbm.at[:, at], v.at[:, at], sems.at[2, j]),
            ]
        )
        for copy in copies[-1]:
            copy.start()
    ordered[...] = gather_points(rows_ref[:RHS], rows_ref[RHS : RHS + 1])
    half = 2 * LANES
    for j in range(CHUNKS):
        for copy in copies[j]:
            copy.wait()
        lo, hi = j * width, (j + 1) * width
        current = jnp.dot(ordered[...], inv[:, lo:hi], preferred_element_type=F32)
        cur_ref[:, lo:hi] = current
        rounded = current.astype(BF16)
        left = lax.dot_general(
            jnp.concatenate([rounded, v[:half, lo:hi]], axis=0), u[:half, lo:hi], NT, preferred_element_type=F32
        )
        right = lax.dot_general(
            jnp.concatenate([rounded, v[:, lo:hi]], axis=0), u[half:, lo:hi], NT, preferred_element_type=F32
        )
        if j == 0:
            proj[:, :half] = left[:RHS]
            proj[:, half:] = right[:RHS]
            gram[:half, :half] = left[RHS:]
            gram[:, half:] = right[RHS:]
        else:
            proj[:, :half] += left[:RHS]
            proj[:, half:] += right[:RHS]
            gram[:half, :half] += left[RHS:]
            gram[:, half:] += right[RHS:]

    right_half = lanes(RANK) >= RANK

    def tile(a, b):
        return gram[a * LANES : (a + 1) * LANES, b * LANES : (b + 1) * LANES]

    def diag(a):
        return jnp.where(right_half, gram[a * LANES : a * LANES + RANK, a * LANES : (a + 1) * LANES], 0.0)

    pay_ref[:RHS] = proj[:, :LANES]
    pay_ref[RHS:] = diag(0)
    for b in range(1, PAIRS):
        rest_ref[(b - 1) * RHS : b * RHS] = proj[:, b * LANES : (b + 1) * LANES]
        near_ref[(b - 1) * LANES : b * LANES] = tile(0, b)
    rest_ref[(PAIRS - 1) * RHS :] = diag(1)
    own = bit(0)
    tail = jnp.concatenate([tile(2, 3), jnp.where(right_half, diag(3), swap(diag(2)))], axis=0)
    cut = tail.shape[0] // 2
    halves = [jnp.concatenate([tile(1, 2), tail[:cut]], axis=0), jnp.concatenate([tile(1, 3), tail[cut:]], axis=0)]
    keep_ref[...], send_ref[...] = order(0, *halves)


def pack_kernel(pay_ref, core_ref, out_ref):
    out_ref[:RHS] = pay_ref[:RHS]
    out_ref[RHS : RHS + RANK] = core_ref[0].astype(F32)
    out_ref[RHS + RANK :] = pay_ref[RHS:]


def first_kernel(got_ref, rest_ref, near_ref, core_ref, w_ref, out_ref):
    own = lax.axis_index("leaf") & 3
    weights, after = [], []
    for m in (0, 2):
        pair = [got_ref[m, :RHS], got_ref[m + 1, :RHS]]
        stacked = side_by_side(0, *pair)
        for n in (0, 1):
            weights.append(core_times(stacked, got_ref[m + n, RHS : RHS + RANK].astype(BF16)))
            pair[n] = pair[n] - times(weights[-1], got_ref[m + n, RHS + RANK :])
        after.append(pair[0] + pair[1])
    second = core_times(side_by_side(1, *after), core_ref[0])
    first = jnp.zeros((RHS, RANK), F32)
    for n in range(4):
        first = jnp.where(own == n, weights[n].astype(F32), first)
    w_ref[:, :RANK] = first
    w_ref[:, RANK:] = second.astype(F32)
    both = w_ref[...].astype(BF16)
    for i in range(PAIRS - 1):
        rows = slice(i * RHS, (i + 1) * RHS)
        out_ref[rows] = rest_ref[rows] - times(both, near_ref[i * LANES : (i + 1) * LANES])
    out_ref[(PAIRS - 1) * RHS :] = rest_ref[(PAIRS - 1) * RHS :]


def node_kernel(got_ref, core_ref, pay_ref, keep_ref):
    total = (got_ref[0] + got_ref[1]) + (got_ref[2] + got_ref[3])
    pay_ref[:RHS] = total[:RHS]
    pay_ref[RHS : RHS + RANK] = core_ref[0].astype(F32)
    pay_ref[RHS + RANK :] = total[(PAIRS - 1) * RHS :]
    keep_ref[...] = total[RHS : (PAIRS - 1) * RHS]


def level2_kernel(own_ref, far_ref, w_ref, out_ref):
    own, far = own_ref[:RHS], far_ref[:RHS]
    cores = slice(RHS, RHS + RANK)
    both = both_weights(2, own, far, own_ref[cores], far_ref[cores])
    w_ref[...] = both.astype(F32)
    diag = jnp.concatenate([own_ref[RHS + RANK :], far_ref[RHS + RANK :]], axis=0)
    out_ref[...] = (own + far) - times(both, diag)


def level3_kernel(own_ref, far_ref, core_ref, w2_ref, keep_ref, near_ref, far_near_ref, w_ref, out_ref):
    stacked = side_by_side(3, *order(3, own_ref[...], far_ref[...]))
    w_ref[:, :RANK] = w2_ref[:, :RANK]
    w_ref[:, RANK:] = core_times(stacked, core_ref[0]).astype(F32)
    both = w_ref[...].astype(BF16)
    for i, product in enumerate(order(0, near_ref[...], far_near_ref[...])):
        rows = slice(i * RHS, (i + 1) * RHS)
        out_ref[rows] = keep_ref[rows] - times(both, product)


def add_kernel(a_ref, b_ref, out_ref):
    out_ref[...] = a_ref[...] + b_ref[...]


def late_kernel(a_ref, b_ref, after_ref, out_ref):
    out_ref[...] = a_ref[...] + b_ref[...]


def take_kernel(a_ref, b_ref, after_ref, near_ref, out_ref):
    rows = near_ref.shape[0]
    near_ref[...] = a_ref[:rows] + b_ref[:rows]
    out_ref[...] = a_ref[rows:] + b_ref[rows:]


def level4_products(own_ref, far_ref, core_ref, out_ref):
    rows = own_ref.shape[0]
    out_ref[:rows], out_ref[rows : 2 * rows] = order(0, own_ref[...], far_ref[...])
    out_ref[2 * rows :] = core_ref[0].astype(F32)


def level5_products(own_ref, far_ref, after_ref, core_ref, out_ref):
    out_ref[:RANK] = own_ref[RANK:LANES] + far_ref[RANK:LANES]
    total = own_ref[LANES : LANES + RANK] + far_ref[LANES : LANES + RANK]
    out_ref[RANK:LANES] = jnp.where(lanes(RANK) < RANK, 0.0, total)
    out_ref[LANES:] = core_ref[0].astype(F32)


def level6_products(own_ref, far_ref, after_ref, core_ref, out_ref):
    out_ref[:RANK] = own_ref[RANK:LANES] + far_ref[RANK:LANES]
    out_ref[RANK:] = core_ref[0].astype(F32)


def both_weights(k, own, far, core, far_core):
    stacked = side_by_side(k, *order(k, own, far))
    return core_times(stacked, jnp.concatenate([core, far_core], axis=0).astype(BF16))


def level4_kernel(own_ref, far_ref, prod_ref, far_prod_ref, w_ref, out_ref):
    own, far = own_ref[...], far_ref[...]
    both = both_weights(4, own[:RHS], far[:RHS], prod_ref[LANES + RANK :], far_prod_ref[LANES + RANK :])
    w_ref[...] = both.astype(F32)
    cross = jnp.concatenate([prod_ref[:RANK], far_prod_ref[:RANK]], axis=0)
    diag = jnp.concatenate([prod_ref[LANES : LANES + RANK], far_prod_ref[LANES : LANES + RANK]], axis=0)
    diag = jnp.where(lanes(LANES) < RANK, 0.0, swap(diag))
    total = own + far
    out_ref[:RHS] = total[:RHS] - times(both, diag)
    out_ref[RHS:] = total[RHS:] - times(both, cross)


def level5_kernel(own_ref, far_ref, prod_ref, far_prod_ref, w_ref, out_ref):
    both = both_weights(5, own_ref[:RHS], far_ref[:RHS], prod_ref[LANES:], far_prod_ref[LANES:])
    w_ref[...] = both.astype(F32)
    cross = jnp.concatenate([prod_ref[:RANK], far_prod_ref[:RANK]], axis=0)
    out_ref[...] = (own_ref[RHS:] + far_ref[RHS:]) - times(both, cross)


def level6_kernel(own_ref, far_ref, prod_ref, far_prod_ref, w_ref, out_ref):
    both = both_weights(6, own_ref[...], far_ref[...], prod_ref[RANK:], far_prod_ref[RANK:])
    w_ref[...] = both.astype(F32)
    diag = jnp.concatenate([prod_ref[:RANK], far_prod_ref[:RANK]], axis=0)
    out_ref[...] = (own_ref[...] + far_ref[...]) - times(both, diag)


def last_kernel(own_ref, far_ref, core_ref, cur_ref, w01_ref, w23_ref, w4_ref, w5_ref, w6_ref, v_ref, pos_ref, out_ref):
    leaf = cur_ref.shape[1]
    w7 = core_times(side_by_side(7, *order(7, own_ref[...], far_ref[...])), core_ref[0])
    weights = [w01_ref[...].astype(BF16), w23_ref[...].astype(BF16)]
    weights += [w_ref[:, :RANK].astype(BF16) for w_ref in (w4_ref, w5_ref, w6_ref)] + [w7]
    current = cur_ref[...] - jnp.dot(jnp.concatenate(weights, axis=1), v_ref[...], preferred_element_type=F32)
    positions = pos_ref[...]
    high = positions // WIDE
    parts = jnp.concatenate([x.astype(F32) for x in split(current, 2)], axis=0)
    count = leaf // WIDE
    chosen = [jnp.where(high == h, parts, 0.0).astype(BF16) for h in range(count)]
    moved = lax.dot_general(
        jnp.concatenate(chosen, axis=0), one_hot_low(positions, leaf), NT, preferred_element_type=F32
    )
    for h in range(count):
        lo = 2 * RHS * h
        out_ref[:, h * WIDE : (h + 1) * WIDE] = moved[lo : lo + RHS] + moved[lo + RHS : lo + 2 * RHS]


def local(right_sides, point_order, leaf_inverse, test_bases, trial_bases, coupling_cores):
    devices = lax.axis_size("leaf")
    leaf = right_sides.shape[1]
    total = PAIRS * LANES
    test = test_bases.reshape(total, leaf)
    trial = trial_bases.reshape(total, leaf)
    vmem = pl.BlockSpec(memory_space=pltpu.VMEM)
    anywhere = pl.BlockSpec(memory_space=pl.ANY)
    hbm = pl.BlockSpec(memory_space=pltpu.HBM)

    def shape(*dims):
        return jax.ShapeDtypeStruct(dims, F32)

    def core(level):
        return pl.BlockSpec((1, RANK, LANES), lambda *_: (level, 0, 0))

    def call(kernel, name, args, shapes, level=None, at=None, after=None, limit=16):
        specs = [vmem] * len(args)
        grid = {}
        if at is not None:
            specs[at] = core(level)
            grid = {"grid": (1,)}
        if after is not None:
            specs[after] = anywhere
        return pl.pallas_call(
            kernel,
            in_specs=specs,
            out_specs=[vmem] * len(shapes),
            out_shape=shapes,
            compiler_params=pltpu.CompilerParams(vmem_limit_bytes=limit * 2**20),
            name=name,
            **grid,
        )(*args)

    def pair(values, k):
        return lax.ppermute(values, "leaf", [(d, d ^ 1 << k) for d in range(devices)])

    near_four = [[4 * n + i for i in range(4)] for n in range(devices // 4)]

    def four(values):
        return lax.all_gather(values, "leaf", axis=0, axis_index_groups=near_four)

    cores = coupling_cores
    tail = (LANES + RANK) // 2
    late_rows = LANES + tail
    rows = jnp.concatenate([right_sides.astype(F32), point_order.astype(F32), jnp.zeros((7, leaf), F32)], axis=0)
    current, pay, rest, near, late, late_send = pl.pallas_call(
        front_kernel,
        in_specs=[vmem, anywhere, anywhere, anywhere],
        out_specs=[vmem] * 6,
        out_shape=[
            shape(RHS, leaf),
            shape(RHS + RANK, LANES),
            shape((PAIRS - 1) * RHS + RANK, LANES),
            shape((PAIRS - 1) * LANES, LANES),
            shape(late_rows, LANES),
            shape(late_rows, LANES),
        ],
        scratch_shapes=[
            pltpu.VMEM((leaf, leaf), BF16),
            pltpu.VMEM((total, leaf), BF16),
            pltpu.VMEM((total, leaf), BF16),
            pltpu.VMEM((RHS, leaf), BF16),
            pltpu.VMEM((RHS, total), F32),
            pltpu.VMEM((total, total), F32),
            pltpu.SemaphoreType.DMA((3, CHUNKS)),
        ],
        compiler_params=pltpu.CompilerParams(vmem_limit_bytes=52 * 2**20),
        name="front",
    )(rows, leaf_inverse, test, trial)
    (pay,) = call(pack_kernel, "pack", (pay, cores), [shape(MESSAGE, LANES)], level=0, at=1)

    one = shape(RHS, LANES)
    two = shape(2 * RHS, LANES)

    late_far = pair(late_send, 0)
    got = four(pay)
    (late,) = call(late_kernel, "late0", (late, late_far, got), [shape(late_rows, LANES)], after=2)
    late_far = pair(late, 1)
    w01, rest = call(first_kernel, "first", (got, rest, near, cores), [one, shape(*rest.shape)], level=1, at=3)
    pay, keep = call(node_kernel, "node", (four(rest), cores), [shape(MESSAGE, LANES), two], level=2, at=1)
    pay_far = pair(pay, 2)
    near, prod = call(take_kernel, "late1", (late, late_far, pay), [shape(LANES, LANES), shape(tail, LANES)], after=2)
    near_far = pair(near, 0)
    prod_far = pair(prod, 2)
    w2, half = call(level2_kernel, "level2", (pay, pay_far), [one, one])
    half_far = pair(half, 3)
    w23, keep = call(
        level3_kernel, "level3", (half, half_far, cores, w2, keep, near, near_far), [one, two], level=3, at=2
    )
    keep_far = pair(keep, 2)
    (prod,) = call(late_kernel, "late2", (prod, prod_far, half_far), [shape(tail, LANES)], after=2)
    prod_far = pair(prod, 3)
    (keep,) = call(add_kernel, "sum2", (keep, keep_far), [two])
    keep_far = pair(keep, 3)
    (prod,) = call(late_kernel, "late3", (prod, prod_far, keep), [shape(tail, LANES)], after=2)
    (prod4,) = call(level4_products, "both", (prod, pair(prod, 0), cores), [shape(2 * LANES, LANES)], level=4, at=2)
    far4 = pair(prod4, 4)
    (keep,) = call(add_kernel, "sum3", (keep, keep_far), [two])
    keep_far = pair(keep, 4)
    w4, keep = call(level4_kernel, "level4", (keep, keep_far, prod4, far4), [one, two])
    (prod5,) = call(
        level5_products, "late4", (prod4, far4, w4, cores), [shape(3 * RANK, LANES)], level=5, at=3, after=2
    )
    far5 = pair(prod5, 5)
    w5, keep = call(level5_kernel, "level5", (keep, pair(keep, 5), prod5, far5), [one, one])
    (prod6,) = call(
        level6_products, "late5", (prod5, far5, w5, cores), [shape(2 * RANK, LANES)], level=6, at=3, after=2
    )
    far6 = pair(prod6, 6)
    w6, keep = call(level6_kernel, "level6", (keep, pair(keep, 6), prod6, far6), [one, one])
    return call(
        last_kernel,
        "last",
        (keep, pair(keep, 7), cores, current, w01, w23, w4, w5, w6, trial, point_order),
        [shape(RHS, leaf)],
        level=7,
        at=2,
        limit=32,
    )[0]


def solution(mesh):
    in_specs = (
        P(None, "leaf"),
        P("leaf", None),
        P("leaf", None),
        P(None, None, "leaf"),
        P(None, None, "leaf"),
        P(None, "leaf", None),
    )
    out_specs = P(None, "leaf")
    return jax.shard_map(local, mesh=mesh, in_specs=in_specs, out_specs=out_specs, check_vma=False)
```

```python
import functools

import jax
import jax.numpy as jnp
from jax import lax
from jax.experimental import pallas as pl
from jax.experimental.pallas import tpu as pltpu
from jax.sharding import PartitionSpec as P


F32 = jnp.float32
BF16 = jnp.bfloat16
PAIRS = 4
RHS = 16
RANK = 64
LANES = 128
WIDE = 256
CHUNKS = 4
NT = (((1,), (1,)), ((), ()))
PAY = RHS + RANK // 2


def split(x, parts):
    out = []
    for _ in range(parts):
        piece = x.astype(BF16)
        out.append(piece)
        x = x - piece.astype(F32)
    return out


def times(weights, product):
    high, low = split(product, 2)
    return jnp.dot(weights, high, preferred_element_type=F32) + jnp.dot(weights, low, preferred_element_type=F32)


def core_times(stacked, cores):
    rows = stacked.shape[0]
    out = lax.dot_general(jnp.concatenate(split(stacked, 3), axis=0), cores, NT, preferred_element_type=F32)
    return (out[:rows] + (out[rows : 2 * rows] + out[2 * rows :])).astype(BF16)


def lanes(rows=RHS):
    return lax.broadcasted_iota(jnp.int32, (rows, LANES), 1)


def swap(x):
    return pltpu.roll(x, RANK, 1)


def bit(k):
    return lax.axis_index("leaf") >> k & 1


def order(k, own, far):
    upper = bit(k) == 1
    return jnp.where(upper, far, own), jnp.where(upper, own, far)


def side_by_side(k, low, high):
    if k % 2:
        return jnp.where(lanes() < RANK, swap(low), high)
    return jnp.where(lanes() < RANK, low, swap(high))


def one_hot_low(positions, leaf):
    rows = lax.broadcasted_iota(jnp.int32, (WIDE, leaf), 0)
    return jnp.where(rows == (positions & (WIDE - 1)), 1.0, 0.0).astype(BF16)


def gather_points(sides, positions):
    leaf = sides.shape[1]
    high = positions // WIDE
    rows = jnp.concatenate([sides[:, h * WIDE : (h + 1) * WIDE] for h in range(leaf // WIDE)], axis=0)
    picked = jnp.dot(rows, one_hot_low(positions, leaf), preferred_element_type=F32)
    total = jnp.zeros((RHS, leaf), F32)
    for h in range(leaf // WIDE):
        total = total + jnp.where(high == h, picked[h * RHS : (h + 1) * RHS], 0.0)
    return total.astype(BF16)


def chunked(leaf, pairs, sems):
    width = leaf // CHUNKS
    copies = []
    for j in range(CHUNKS):
        at = pl.ds(j * width, width)
        copies.append(
            [pltpu.make_async_copy(src.at[:, at], dst.at[:, at], sems.at[i, j]) for i, (src, dst) in enumerate(pairs)]
        )
        for copy in copies[-1]:
            copy.start()
    return copies


def pack(right):
    half = RANK // 2
    return jnp.where(lanes(half) < RANK, swap(right[:half]), right[half:])


def unpack(rows):
    both = jnp.concatenate([swap(rows), rows], axis=0)
    return jnp.where(lanes(RANK) < RANK, 0.0, both)


def leaf_kernel(
    rs_ref, pos_ref, inv_hbm, u_hbm, v_hbm, cur_ref, pay_ref, rest_ref, near_ref, inv, u, v, ordered, both, sems
):
    leaf = rs_ref.shape[1]
    width = leaf // CHUNKS
    copies = chunked(leaf, [(inv_hbm, inv), (u_hbm, u), (v_hbm.at[:LANES], v)], sems)
    ordered[...] = gather_points(rs_ref[...], pos_ref[...])
    for j in range(CHUNKS):
        for copy in copies[j]:
            copy.wait()
        lo, hi = j * width, (j + 1) * width
        current = jnp.dot(ordered[...], inv[:, lo:hi], preferred_element_type=F32)
        cur_ref[:, lo:hi] = current
        rows = jnp.concatenate([current.astype(BF16), v[:, lo:hi]], axis=0)
        part = lax.dot_general(rows, u[:, lo:hi], NT, preferred_element_type=F32)
        if j == 0:
            both[...] = part
        else:
            both[...] += part
    pay_ref[:RHS] = both[:RHS, :LANES]
    pay_ref[RHS:] = pack(both[RHS : RHS + RANK, :LANES])
    for b in range(1, PAIRS):
        rest_ref[(b - 1) * RHS : b * RHS] = both[:RHS, b * LANES : (b + 1) * LANES]
        near_ref[(b - 1) * LANES : b * LANES] = both[RHS:, b * LANES : (b + 1) * LANES]


def products_kernel(u_hbm, v_hbm, diag_ref, keep_ref, send_ref, u, v, gram, sems):
    leaf = u.shape[1]
    width = leaf // CHUNKS
    copies = chunked(leaf, [(u_hbm.at[LANES:], u), (v_hbm.at[LANES:], v)], sems)
    for j in range(CHUNKS):
        for copy in copies[j]:
            copy.wait()
        lo, hi = j * width, (j + 1) * width
        part = lax.dot_general(v[:, lo:hi], u[:, lo:hi], NT, preferred_element_type=F32)
        if j == 0:
            gram[...] = part
        else:
            gram[...] += part

    def tile(a, b):
        return gram[(a - 1) * LANES : a * LANES, (b - 1) * LANES : b * LANES]

    diag_ref[...] = pack(tile(1, 1)[:RANK])
    diag = jnp.where(lanes(RANK) < RANK, swap(tile(2, 2)[:RANK]), tile(3, 3)[:RANK])
    tail = jnp.concatenate([tile(2, 3), diag], axis=0)
    cut = tail.shape[0] // 2
    halves = [jnp.concatenate([tile(1, 2), tail[:cut]], axis=0), jnp.concatenate([tile(1, 3), tail[cut:]], axis=0)]
    keep_ref[...], send_ref[...] = order(0, *halves)


def first_kernel(pay_ref, core_ref, out_ref):
    rows = pay_ref.shape[0]
    out_ref[:rows] = pay_ref[...]
    out_ref[rows:] = core_ref[0].astype(F32)


def even_step(k, own_ref, far_ref, w_ref, out_ref):
    own, far = own_ref[:RHS], far_ref[:RHS]
    both = both_weights(k, own, far, own_ref[PAY:], far_ref[PAY:])
    w_ref[...] = both.astype(F32)
    at = slice(RHS, PAY)
    diag = jnp.concatenate([unpack(own_ref[at]), unpack(far_ref[at])], axis=0)
    out_ref[...] = (own + far) - times(both, diag)


def level0_kernel(own_ref, far_ref, w_ref, out_ref):
    even_step(0, own_ref, far_ref, w_ref, out_ref)


def level2_kernel(own_ref, far_ref, w_ref, out_ref):
    even_step(2, own_ref, far_ref, w_ref, out_ref)


def odd_weights(k, own_ref, far_ref, core_ref, even_ref, w_ref):
    stacked = side_by_side(k, *order(k, own_ref[...], far_ref[...]))
    w_ref[:, :RANK] = even_ref[:, :RANK]
    w_ref[:, RANK:] = core_times(stacked, core_ref[0]).astype(F32)
    return w_ref[...].astype(BF16)


def level1_kernel(own_ref, far_ref, core_ref, even_ref, rest_ref, near_ref, diag_ref, w_ref, out_ref):
    both = odd_weights(1, own_ref, far_ref, core_ref, even_ref, w_ref)
    later = PAIRS - 1
    for i in range(later):
        rows = slice(i * RHS, (i + 1) * RHS)
        out_ref[rows] = rest_ref[rows] - times(both, near_ref[i * LANES : (i + 1) * LANES])
    out_ref[later * RHS :] = diag_ref[...]


def node_kernel(own_ref, far_ref, core_ref, pay_ref, keep_ref):
    total = own_ref[...] + far_ref[...]
    later = PAIRS - 1
    pay_ref[:RHS] = total[:RHS]
    pay_ref[RHS:PAY] = total[later * RHS :]
    pay_ref[PAY:] = core_ref[0].astype(F32)
    keep_ref[...] = total[RHS : later * RHS]


def level3_kernel(own_ref, far_ref, core_ref, even_ref, keep_ref, near_ref, far_near_ref, w_ref, out_ref):
    both = odd_weights(3, own_ref, far_ref, core_ref, even_ref, w_ref)
    for i, product in enumerate(order(0, near_ref[...], far_near_ref[...])):
        rows = slice(i * RHS, (i + 1) * RHS)
        out_ref[rows] = keep_ref[rows] - times(both, product)


def add_kernel(a_ref, b_ref, out_ref):
    out_ref[...] = a_ref[...] + b_ref[...]


def copy_kernel(a_ref, out_ref):
    out_ref[...] = a_ref[...]


def add_core_kernel(a_ref, b_ref, core_ref, out_ref):
    rows = a_ref.shape[0]
    out_ref[:rows] = a_ref[...] + b_ref[...]
    out_ref[rows:] = core_ref[0].astype(F32)


def take_kernel(a_ref, b_ref, near_ref, out_ref):
    rows = near_ref.shape[0]
    near_ref[...] = a_ref[:rows] + b_ref[:rows]
    out_ref[...] = a_ref[rows:] + b_ref[rows:]


def both_weights(k, own, far, core, far_core):
    stacked = side_by_side(k, *order(k, own, far))
    return core_times(stacked, jnp.concatenate([core, far_core], axis=0).astype(BF16))


def level4_kernel(
    own_ref, far_ref, prod_ref, prod_near_ref, far_prod_ref, far_near_ref, core_ref, w_ref, out_ref
):
    own, far = own_ref[...], far_ref[...]
    rows = prod_ref.shape[0] - RANK
    both = both_weights(4, own[:RHS], far[:RHS], prod_ref[rows:], far_prod_ref[rows:])
    w_ref[...] = both.astype(F32)
    mine = jnp.concatenate(order(0, prod_ref[:rows], prod_near_ref[:rows]), axis=0)
    theirs = jnp.concatenate(order(0, far_prod_ref[:rows], far_near_ref[:rows]), axis=0)
    cross = jnp.concatenate([mine[:RANK], theirs[:RANK]], axis=0)
    diag = jnp.concatenate([mine[LANES:], theirs[LANES:]], axis=0)
    diag = jnp.where(lanes(LANES) < RANK, 0.0, swap(diag))
    total = own + far
    out_ref[:RHS] = total[:RHS] - times(both, diag)
    out_ref[RHS : 2 * RHS] = total[RHS:] - times(both, cross)
    later = mine[RANK:] + theirs[RANK:]
    out_ref[2 * RHS : 2 * RHS + RANK] = later[:RANK]
    out_ref[2 * RHS + RANK : 2 * RHS + RANK + RANK // 2] = pack(later[RANK:])
    out_ref[2 * RHS + RANK + RANK // 2 :] = core_ref[0].astype(F32)


def level5_kernel(own_ref, far_ref, core_ref, w_ref, out_ref):
    cores = slice(2 * RHS + RANK + RANK // 2, own_ref.shape[0])
    both = both_weights(5, own_ref[:RHS], far_ref[:RHS], own_ref[cores], far_ref[cores])
    w_ref[...] = both.astype(F32)
    at = slice(2 * RHS, 2 * RHS + RANK)
    cross = jnp.concatenate([own_ref[at], far_ref[at]], axis=0)
    out_ref[:RHS] = (own_ref[RHS : 2 * RHS] + far_ref[RHS : 2 * RHS]) - times(both, cross)
    at = slice(2 * RHS + RANK, 2 * RHS + RANK + RANK // 2)
    out_ref[RHS:PAY] = own_ref[at] + far_ref[at]
    out_ref[PAY:] = core_ref[0].astype(F32)


def level6_kernel(own_ref, far_ref, w_ref, out_ref):
    even_step(6, own_ref, far_ref, w_ref, out_ref)


def scatter_points(values, positions):
    leaf = positions.shape[1]
    high = positions // WIDE
    count = leaf // WIDE
    parts = jnp.concatenate([x.astype(F32) for x in values], axis=0)
    rows = parts.shape[0]
    chosen = jnp.concatenate([jnp.where(high == h, parts, 0.0).astype(BF16) for h in range(count)], axis=0)
    moved = lax.dot_general(chosen, one_hot_low(positions, leaf), NT, preferred_element_type=F32)
    return [moved[h * rows : (h + 1) * rows] for h in range(count)]


def place_kernel(cur_ref, w01_ref, w23_ref, w4_ref, w5_ref, w6_ref, v_ref, pos_ref, out_ref, basis_ref):
    weights = [w01_ref[...].astype(BF16), w23_ref[...].astype(BF16)]
    weights += [w_ref[:, :RANK].astype(BF16) for w_ref in (w4_ref, w5_ref, w6_ref)]
    known = v_ref.shape[0] - RANK
    current = cur_ref[...] - jnp.dot(jnp.concatenate(weights, axis=1), v_ref[:known], preferred_element_type=F32)
    for h, block in enumerate(scatter_points(split(current, 2) + [v_ref[known:]], pos_ref[...])):
        at = slice(h * WIDE, (h + 1) * WIDE)
        out_ref[:, at] = block[:RHS] + block[RHS : 2 * RHS]
        basis_ref[:, at] = block[2 * RHS :].astype(BF16)


def last_kernel(own_ref, far_ref, core_ref, placed_ref, basis_ref, out_ref):
    weights = core_times(side_by_side(7, *order(7, own_ref[...], far_ref[...])), core_ref[0])
    out_ref[...] = placed_ref[...] - jnp.dot(weights, basis_ref[...], preferred_element_type=F32)


def local(right_sides, point_order, leaf_inverse, test_bases, trial_bases, coupling_cores):
    devices = lax.axis_size("leaf")
    leaf = right_sides.shape[1]
    total = PAIRS * LANES
    test = test_bases.reshape(total, leaf)
    trial = trial_bases.reshape(total, leaf)
    vmem = pl.BlockSpec(memory_space=pltpu.VMEM)
    anywhere = pl.BlockSpec(memory_space=pl.ANY)
    hbm = pl.BlockSpec(memory_space=pltpu.HBM)

    def shape(*dims):
        return jax.ShapeDtypeStruct(dims, F32)

    def core(level):
        return pl.BlockSpec((1, RANK, LANES), lambda *_: (level, 0, 0))

    def call(kernel, name, args, shapes, level=None, at=None, after=(), limit=16, hint=0):
        count = len(args)
        specs = [vmem] * count + [anywhere] * len(after)
        grid = {}
        if at is not None:
            specs[at] = core(level)
            grid = {"grid": (1,)}

        def body(*refs):
            kernel(*refs[:count], *refs[count + len(after) :])

        return pl.pallas_call(
            body,
            in_specs=specs,
            out_specs=[vmem] * len(shapes),
            out_shape=shapes,
            compiler_params=pltpu.CompilerParams(vmem_limit_bytes=limit * 2**20),
            name=name,
            cost_estimate=pl.CostEstimate(flops=hint, bytes_accessed=0, transcendentals=0) if hint else None,
            **grid,
        )(*args, *after)

    main = functools.partial(call, hint=int(6e9))

    def pair(values, k):
        mask = {3: 3 << 2, 5: 3 << 4, 7: 3 << 6}.get(k, 1 << k)
        return lax.ppermute(values, "leaf", [(d, d ^ mask) for d in range(devices)])

    cores = coupling_cores
    tail = (LANES + RANK) // 2
    late_rows = LANES + tail
    later_rows = (PAIRS - 1) * RHS
    big = pltpu.CompilerParams(vmem_limit_bytes=52 * 2**20)
    current, pay, rest, near = pl.pallas_call(
        leaf_kernel,
        in_specs=[vmem, vmem, anywhere, anywhere, anywhere],
        out_specs=[vmem] * 4,
        out_shape=[
            shape(RHS, leaf),
            shape(PAY, LANES),
            shape(later_rows, LANES),
            shape((PAIRS - 1) * LANES, LANES),
        ],
        scratch_shapes=[
            pltpu.VMEM((leaf, leaf), BF16),
            pltpu.VMEM((total, leaf), BF16),
            pltpu.VMEM((LANES, leaf), BF16),
            pltpu.VMEM((RHS, leaf), BF16),
            pltpu.VMEM((RHS + LANES, total), F32),
            pltpu.SemaphoreType.DMA((3, CHUNKS)),
        ],
        compiler_params=big,
        name="leaf",
    )(right_sides, point_order, leaf_inverse, test, trial)

    one = shape(RHS, LANES)
    two = shape(2 * RHS, LANES)

    (pay,) = call(first_kernel, "first", (pay, cores), [shape(PAY + RANK, LANES)], 0, 1)
    w0, half = main(level0_kernel, "level0", (pay, pair(pay, 0)), [one, one])
    half_far = pair(half, 1)

    def products_body(after_ref, *refs):
        products_kernel(*refs)

    diag, late, late_send = pl.pallas_call(
        products_body,
        in_specs=[anywhere] * 3,
        out_specs=[vmem] * 3,
        out_shape=[shape(RANK // 2, LANES), shape(late_rows, LANES), shape(late_rows, LANES)],
        scratch_shapes=[
            pltpu.VMEM((total - LANES, leaf), BF16),
            pltpu.VMEM((total - LANES, leaf), BF16),
            pltpu.VMEM((total - LANES, total - LANES), F32),
            pltpu.SemaphoreType.DMA((2, CHUNKS)),
        ],
        compiler_params=big,
        cost_estimate=pl.CostEstimate(flops=2 * leaf * (total - LANES) ** 2, bytes_accessed=4 * leaf * (total - LANES), transcendentals=0),
        name="products",
    )(half, test, trial)
    late_far = pair(late_send, 0)
    w01, rest = main(
        level1_kernel,
        "level1",
        (half, half_far, cores, w0, rest, near, diag),
        [one, shape(later_rows + RANK // 2, LANES)],
        1,
        2,
    )
    rest_far = pair(rest, 0)
    (late,) = call(add_kernel, "late0", (late, late_far), [shape(late_rows, LANES)], after=(w01,))
    late_far = pair(late, 1)
    (rest,) = main(add_kernel, "sum0", (rest, rest_far), [shape(later_rows + RANK // 2, LANES)])
    rest_far = pair(rest, 1)
    pay, keep = main(node_kernel, "node", (rest, rest_far, cores), [shape(PAY + RANK, LANES), two], 2, 2)
    pay_far = pair(pay, 2)
    near, prod = call(take_kernel, "late1", (late, late_far), [shape(LANES, LANES), shape(tail, LANES)], after=(rest,))
    near_far = pair(near, 0)
    prod_far = pair(prod, 2)
    w2, half = main(level2_kernel, "level2", (pay, pay_far), [one, one])
    half_far = pair(half, 3)
    (prod,) = call(add_kernel, "late2", (prod, prod_far), [shape(tail, LANES)], after=(half_far,))
    prod_far = pair(prod, 3)
    w23, keep = main(
        level3_kernel, "level3", (half, half_far, cores, w2, keep, near, near_far), [one, two], 3, 2
    )
    keep_far = pair(keep, 2)
    (keep,) = main(add_kernel, "sum2", (keep, keep_far), [two])
    keep_far = pair(keep, 3)
    (prod,) = call(add_core_kernel, "late3", (prod, prod_far, cores), [shape(tail + RANK, LANES)], 4, 2, (keep,))
    prod_near, far_prod = pair(prod, 0), pair(prod, 4)
    (keep,) = main(add_kernel, "sum3", (keep, keep_far), [two])
    keep_far = pair(keep, 4)
    (far_copy,) = call(copy_kernel, "late4", (far_prod,), [shape(*far_prod.shape)], after=(keep,))
    w4, keep = main(
        level4_kernel,
        "level4",
        (keep, keep_far, prod, prod_near, far_prod, pair(far_copy, 0), cores),
        [one, shape(2 * RHS + 2 * RANK + RANK // 2, LANES)],
        5,
        6,
    )
    w5, keep = main(level5_kernel, "level5", (keep, pair(keep, 5), cores), [one, shape(PAY + RANK, LANES)], 6, 2)
    w6, keep = main(level6_kernel, "level6", (keep, pair(keep, 6)), [one, one])
    keep_far = pair(keep, 7)
    placed, basis = call(
        place_kernel,
        "place",
        (current, w01, w23, w4, w5, w6, trial, point_order),
        [shape(RHS, leaf), jax.ShapeDtypeStruct((RANK, leaf), BF16)],
        limit=32,
    )
    return call(
        last_kernel, "last", (keep, keep_far, cores, placed, basis), [shape(RHS, leaf)], level=7, at=2
    )[0]


def solution(mesh):
    in_specs = (
        P(None, "leaf"),
        P("leaf", None),
        P("leaf", None),
        P(None, None, "leaf"),
        P(None, None, "leaf"),
        P(None, "leaf", None),
    )
    out_specs = P(None, "leaf")
    return jax.shard_map(local, mesh=mesh, in_specs=in_specs, out_specs=out_specs, check_vma=False)
```

```python
import functools

import jax
import jax.numpy as jnp
from jax import lax
from jax.experimental import pallas as pl
from jax.experimental.pallas import tpu as pltpu
from jax.sharding import PartitionSpec as P


F32 = jnp.float32
BF16 = jnp.bfloat16
PAIRS = 4
RHS = 16
RANK = 64
LANES = 128
WIDE = 256
CHUNKS = 4
NT = (((1,), (1,)), ((), ()))
PAY = RHS + RANK // 2


def split(x, parts):
    out = []
    for _ in range(parts):
        piece = x.astype(BF16)
        out.append(piece)
        x = x - piece.astype(F32)
    return out


def times(weights, product):
    high, low = split(product, 2)
    return jnp.dot(weights, high, preferred_element_type=F32) + jnp.dot(weights, low, preferred_element_type=F32)


def core_times(stacked, cores):
    rows = stacked.shape[0]
    out = lax.dot_general(jnp.concatenate(split(stacked, 3), axis=0), cores, NT, preferred_element_type=F32)
    return (out[:rows] + (out[rows : 2 * rows] + out[2 * rows :])).astype(BF16)


def lanes(rows=RHS):
    return lax.broadcasted_iota(jnp.int32, (rows, LANES), 1)


def swap(x):
    return pltpu.roll(x, RANK, 1)


def bit(k):
    return lax.axis_index("leaf") >> k & 1


def order(k, own, far):
    upper = bit(k) == 1
    return jnp.where(upper, far, own), jnp.where(upper, own, far)


def side_by_side(k, low, high):
    if k % 2:
        return jnp.where(lanes() < RANK, swap(low), high)
    return jnp.where(lanes() < RANK, low, swap(high))


def one_hot_low(positions, leaf):
    rows = lax.broadcasted_iota(jnp.int32, (WIDE, leaf), 0)
    return jnp.where(rows == (positions & (WIDE - 1)), 1.0, 0.0).astype(BF16)


def gather_points(sides, positions):
    leaf = sides.shape[1]
    high = positions // WIDE
    rows = jnp.concatenate([sides[:, h * WIDE : (h + 1) * WIDE] for h in range(leaf // WIDE)], axis=0)
    picked = jnp.dot(rows, one_hot_low(positions, leaf), preferred_element_type=F32)
    total = jnp.zeros((RHS, leaf), F32)
    for h in range(leaf // WIDE):
        total = total + jnp.where(high == h, picked[h * RHS : (h + 1) * RHS], 0.0)
    return total.astype(BF16)


def chunked(leaf, pairs, sems):
    width = leaf // CHUNKS
    copies = []
    for j in range(CHUNKS):
        at = pl.ds(j * width, width)
        copies.append(
            [pltpu.make_async_copy(src.at[:, at], dst.at[:, at], sems.at[i, j]) for i, (src, dst) in enumerate(pairs)]
        )
        for copy in copies[-1]:
            copy.start()
    return copies


def pack(right):
    half = RANK // 2
    return jnp.where(lanes(half) < RANK, swap(right[:half]), right[half:])


def unpack(rows):
    both = jnp.concatenate([swap(rows), rows], axis=0)
    return jnp.where(lanes(RANK) < RANK, 0.0, both)


def ready_kernel(out_ref):
    out_ref[...] = jnp.zeros_like(out_ref)


def leaf_kernel(
    rs_ref, pos_ref, inv_hbm, u_hbm, v_hbm, cur_ref, pay_ref, rest_ref, near_ref, inv, u, v, ordered, both, sems
):
    leaf = rs_ref.shape[1]
    width = leaf // CHUNKS
    copies = chunked(leaf, [(inv_hbm, inv), (u_hbm, u), (v_hbm.at[:LANES], v)], sems)
    ordered[...] = gather_points(rs_ref[...], pos_ref[...])
    for j in range(CHUNKS):
        for copy in copies[j]:
            copy.wait()
        lo, hi = j * width, (j + 1) * width
        current = jnp.dot(ordered[...], inv[:, lo:hi], preferred_element_type=F32)
        cur_ref[:, lo:hi] = current
        rows = jnp.concatenate([current.astype(BF16), v[:, lo:hi]], axis=0)
        part = lax.dot_general(rows, u[:, lo:hi], NT, preferred_element_type=F32)
        if j == 0:
            both[...] = part
        else:
            both[...] += part
    pay_ref[:RHS] = both[:RHS, :LANES]
    pay_ref[RHS:] = pack(both[RHS : RHS + RANK, :LANES])
    for b in range(1, PAIRS):
        rest_ref[(b - 1) * RHS : b * RHS] = both[:RHS, b * LANES : (b + 1) * LANES]
        near_ref[(b - 1) * LANES : b * LANES] = both[RHS:, b * LANES : (b + 1) * LANES]


def products_kernel(u_hbm, v_hbm, diag_ref, keep_ref, send_ref, u, v, gram, sems):
    leaf = u.shape[1]
    width = leaf // CHUNKS
    copies = chunked(leaf, [(u_hbm.at[LANES:], u), (v_hbm.at[LANES:], v)], sems)
    for j in range(CHUNKS):
        for copy in copies[j]:
            copy.wait()
        lo, hi = j * width, (j + 1) * width
        part = lax.dot_general(v[:, lo:hi], u[:, lo:hi], NT, preferred_element_type=F32)
        if j == 0:
            gram[...] = part
        else:
            gram[...] += part

    def tile(a, b):
        return gram[(a - 1) * LANES : a * LANES, (b - 1) * LANES : b * LANES]

    diag_ref[...] = pack(tile(1, 1)[:RANK])
    diag = jnp.where(lanes(RANK) < RANK, swap(tile(2, 2)[:RANK]), tile(3, 3)[:RANK])
    tail = jnp.concatenate([tile(2, 3), diag], axis=0)
    cut = tail.shape[0] // 2
    halves = [jnp.concatenate([tile(1, 2), tail[:cut]], axis=0), jnp.concatenate([tile(1, 3), tail[cut:]], axis=0)]
    keep_ref[...], send_ref[...] = order(0, *halves)


def first_kernel(pay_ref, core_ref, out_ref):
    rows = pay_ref.shape[0]
    out_ref[:rows] = pay_ref[...]
    out_ref[rows:] = core_ref[0].astype(F32)


def even_step(k, own_ref, far_ref, w_ref, out_ref):
    own, far = own_ref[:RHS], far_ref[:RHS]
    both = both_weights(k, own, far, own_ref[PAY:], far_ref[PAY:])
    w_ref[...] = both.astype(F32)
    at = slice(RHS, PAY)
    diag = jnp.concatenate([unpack(own_ref[at]), unpack(far_ref[at])], axis=0)
    out_ref[...] = (own + far) - times(both, diag)


def level0_kernel(own_ref, far_ref, w_ref, out_ref):
    even_step(0, own_ref, far_ref, w_ref, out_ref)


def level2_kernel(own_ref, far_ref, w_ref, out_ref):
    even_step(2, own_ref, far_ref, w_ref, out_ref)


def odd_weights(k, own_ref, far_ref, core_ref, even_ref, w_ref):
    stacked = side_by_side(k, *order(k, own_ref[...], far_ref[...]))
    w_ref[:, :RANK] = even_ref[:, :RANK]
    w_ref[:, RANK:] = core_times(stacked, core_ref[0]).astype(F32)
    return w_ref[...].astype(BF16)


def level1_kernel(own_ref, far_ref, core_ref, even_ref, rest_ref, near_ref, diag_ref, w_ref, out_ref):
    both = odd_weights(1, own_ref, far_ref, core_ref, even_ref, w_ref)
    later = PAIRS - 1
    for i in range(later):
        rows = slice(i * RHS, (i + 1) * RHS)
        out_ref[rows] = rest_ref[rows] - times(both, near_ref[i * LANES : (i + 1) * LANES])
    out_ref[later * RHS :] = diag_ref[...]


def node_kernel(own_ref, far_ref, core_ref, pay_ref, keep_ref):
    total = own_ref[...] + far_ref[...]
    later = PAIRS - 1
    pay_ref[:RHS] = total[:RHS]
    pay_ref[RHS:PAY] = total[later * RHS :]
    pay_ref[PAY:] = core_ref[0].astype(F32)
    keep_ref[...] = total[RHS : later * RHS]


def level3_kernel(own_ref, far_ref, core_ref, even_ref, keep_ref, near_ref, far_near_ref, w_ref, out_ref):
    both = odd_weights(3, own_ref, far_ref, core_ref, even_ref, w_ref)
    for i, product in enumerate(order(0, near_ref[...], far_near_ref[...])):
        rows = slice(i * RHS, (i + 1) * RHS)
        out_ref[rows] = keep_ref[rows] - times(both, product)


def add_kernel(a_ref, b_ref, out_ref):
    out_ref[...] = a_ref[...] + b_ref[...]


def copy_kernel(a_ref, out_ref):
    out_ref[...] = a_ref[...]


def add_core_kernel(a_ref, b_ref, core_ref, out_ref):
    rows = a_ref.shape[0]
    out_ref[:rows] = a_ref[...] + b_ref[...]
    out_ref[rows:] = core_ref[0].astype(F32)


def take_kernel(a_ref, b_ref, near_ref, out_ref):
    rows = near_ref.shape[0]
    near_ref[...] = a_ref[:rows] + b_ref[:rows]
    out_ref[...] = a_ref[rows:] + b_ref[rows:]


def both_weights(k, own, far, core, far_core):
    stacked = side_by_side(k, *order(k, own, far))
    return core_times(stacked, jnp.concatenate([core, far_core], axis=0).astype(BF16))


def level4_kernel(
    own_ref, far_ref, prod_ref, prod_near_ref, far_prod_ref, far_near_ref, core_ref, w_ref, out_ref
):
    own, far = own_ref[...], far_ref[...]
    rows = prod_ref.shape[0] - RANK
    both = both_weights(4, own[:RHS], far[:RHS], prod_ref[rows:], far_prod_ref[rows:])
    w_ref[...] = both.astype(F32)
    mine = jnp.concatenate(order(0, prod_ref[:rows], prod_near_ref[:rows]), axis=0)
    theirs = jnp.concatenate(order(0, far_prod_ref[:rows], far_near_ref[:rows]), axis=0)
    cross = jnp.concatenate([mine[:RANK], theirs[:RANK]], axis=0)
    diag = jnp.concatenate([mine[LANES:], theirs[LANES:]], axis=0)
    diag = jnp.where(lanes(LANES) < RANK, 0.0, swap(diag))
    total = own + far
    out_ref[:RHS] = total[:RHS] - times(both, diag)
    out_ref[RHS : 2 * RHS] = total[RHS:] - times(both, cross)
    later = mine[RANK:] + theirs[RANK:]
    out_ref[2 * RHS : 2 * RHS + RANK] = later[:RANK]
    out_ref[2 * RHS + RANK : 2 * RHS + RANK + RANK // 2] = pack(later[RANK:])
    out_ref[2 * RHS + RANK + RANK // 2 :] = core_ref[0].astype(F32)


def level5_kernel(own_ref, far_ref, core_ref, w_ref, out_ref):
    cores = slice(2 * RHS + RANK + RANK // 2, own_ref.shape[0])
    both = both_weights(5, own_ref[:RHS], far_ref[:RHS], own_ref[cores], far_ref[cores])
    w_ref[...] = both.astype(F32)
    at = slice(2 * RHS, 2 * RHS + RANK)
    cross = jnp.concatenate([own_ref[at], far_ref[at]], axis=0)
    out_ref[:RHS] = (own_ref[RHS : 2 * RHS] + far_ref[RHS : 2 * RHS]) - times(both, cross)
    at = slice(2 * RHS + RANK, 2 * RHS + RANK + RANK // 2)
    out_ref[RHS:PAY] = own_ref[at] + far_ref[at]
    out_ref[PAY:] = core_ref[0].astype(F32)


def level6_kernel(own_ref, far_ref, w_ref, out_ref):
    even_step(6, own_ref, far_ref, w_ref, out_ref)


def scatter_points(values, positions):
    leaf = positions.shape[1]
    high = positions // WIDE
    count = leaf // WIDE
    parts = jnp.concatenate([x.astype(F32) for x in values], axis=0)
    rows = parts.shape[0]
    chosen = jnp.concatenate([jnp.where(high == h, parts, 0.0).astype(BF16) for h in range(count)], axis=0)
    moved = lax.dot_general(chosen, one_hot_low(positions, leaf), NT, preferred_element_type=F32)
    return [moved[h * rows : (h + 1) * rows] for h in range(count)]


def place_kernel(cur_ref, w01_ref, w23_ref, w4_ref, w5_ref, w6_ref, v_ref, pos_ref, out_ref, basis_ref):
    weights = [w01_ref[...].astype(BF16), w23_ref[...].astype(BF16)]
    weights += [w_ref[:, :RANK].astype(BF16) for w_ref in (w4_ref, w5_ref, w6_ref)]
    known = v_ref.shape[0] - RANK
    current = cur_ref[...] - jnp.dot(jnp.concatenate(weights, axis=1), v_ref[:known], preferred_element_type=F32)
    for h, block in enumerate(scatter_points(split(current, 2) + [v_ref[known:]], pos_ref[...])):
        at = slice(h * WIDE, (h + 1) * WIDE)
        out_ref[:, at] = block[:RHS] + block[RHS : 2 * RHS]
        basis_ref[:, at] = block[2 * RHS :].astype(BF16)


def last_kernel(own_ref, far_ref, core_ref, placed_ref, basis_ref, out_ref):
    weights = core_times(side_by_side(7, *order(7, own_ref[...], far_ref[...])), core_ref[0])
    out_ref[...] = placed_ref[...] - jnp.dot(weights, basis_ref[...], preferred_element_type=F32)


def local(right_sides, point_order, leaf_inverse, test_bases, trial_bases, coupling_cores):
    devices = lax.axis_size("leaf")
    leaf = right_sides.shape[1]
    total = PAIRS * LANES
    test = test_bases.reshape(total, leaf)
    trial = trial_bases.reshape(total, leaf)
    vmem = pl.BlockSpec(memory_space=pltpu.VMEM)
    anywhere = pl.BlockSpec(memory_space=pl.ANY)
    hbm = pl.BlockSpec(memory_space=pltpu.HBM)

    def shape(*dims):
        return jax.ShapeDtypeStruct(dims, F32)

    def core(level):
        return pl.BlockSpec((1, RANK, LANES), lambda *_: (level, 0, 0))

    def call(kernel, name, args, shapes, level=None, at=None, after=(), limit=16, hint=0):
        count = len(args)
        specs = [vmem] * count + [anywhere] * len(after)
        grid = {}
        if at is not None:
            specs[at] = core(level)
            grid = {"grid": (1,)}

        def body(*refs):
            kernel(*refs[:count], *refs[count + len(after) :])

        return pl.pallas_call(
            body,
            in_specs=specs,
            out_specs=[vmem] * len(shapes),
            out_shape=shapes,
            compiler_params=pltpu.CompilerParams(vmem_limit_bytes=limit * 2**20),
            name=name,
            cost_estimate=pl.CostEstimate(flops=hint, bytes_accessed=0, transcendentals=0) if hint else None,
            **grid,
        )(*args, *after)

    main = functools.partial(call, hint=int(6e9))

    def pair(values, k, across=0):
        mask = {3: 3 << 2, 5: 3 << 4, 7: 3 << 6}.get(k, 1 << k) ^ across
        return lax.ppermute(values, "leaf", [(d, d ^ mask) for d in range(devices)])

    cores = coupling_cores
    tail = (LANES + RANK) // 2
    late_rows = LANES + tail
    later_rows = (PAIRS - 1) * RHS
    big = pltpu.CompilerParams(vmem_limit_bytes=52 * 2**20)
    (ready,) = main(ready_kernel, "ready", (), [shape(8, LANES)])

    def leaf_body(after_ref, *refs):
        leaf_kernel(*refs)

    current, pay, rest, near = pl.pallas_call(
        leaf_body,
        in_specs=[anywhere, vmem, vmem, anywhere, anywhere, anywhere],
        out_specs=[vmem] * 4,
        out_shape=[
            shape(RHS, leaf),
            shape(PAY, LANES),
            shape(later_rows, LANES),
            shape((PAIRS - 1) * LANES, LANES),
        ],
        scratch_shapes=[
            pltpu.VMEM((leaf, leaf), BF16),
            pltpu.VMEM((total, leaf), BF16),
            pltpu.VMEM((LANES, leaf), BF16),
            pltpu.VMEM((RHS, leaf), BF16),
            pltpu.VMEM((RHS + LANES, total), F32),
            pltpu.SemaphoreType.DMA((3, CHUNKS)),
        ],
        compiler_params=big,
        name="leaf",
    )(ready, right_sides, point_order, leaf_inverse, test, trial)

    one = shape(RHS, LANES)
    two = shape(2 * RHS, LANES)

    (pay,) = call(first_kernel, "first", (pay, cores), [shape(PAY + RANK, LANES)], 0, 1)
    w0, half = main(level0_kernel, "level0", (pay, pair(pay, 0)), [one, one])
    half_far = pair(half, 1, 1)

    def products_body(after_ref, *refs):
        products_kernel(*refs)

    diag, late, late_send = pl.pallas_call(
        products_body,
        in_specs=[anywhere] * 3,
        out_specs=[vmem] * 3,
        out_shape=[shape(RANK // 2, LANES), shape(late_rows, LANES), shape(late_rows, LANES)],
        scratch_shapes=[
            pltpu.VMEM((total - LANES, leaf), BF16),
            pltpu.VMEM((total - LANES, leaf), BF16),
            pltpu.VMEM((total - LANES, total - LANES), F32),
            pltpu.SemaphoreType.DMA((2, CHUNKS)),
        ],
        compiler_params=big,
        cost_estimate=pl.CostEstimate(flops=2 * leaf * (total - LANES) ** 2, bytes_accessed=4 * leaf * (total - LANES), transcendentals=0),
        name="products",
    )(half, test, trial)
    late_far = pair(late_send, 0)
    w01, rest = main(
        level1_kernel,
        "level1",
        (half, half_far, cores, w0, rest, near, diag),
        [one, shape(later_rows + RANK // 2, LANES)],
        1,
        2,
    )
    rest_far = pair(rest, 0)
    (late,) = call(add_kernel, "late0", (late, late_far), [shape(late_rows, LANES)], after=(w01,))
    late_far = pair(late, 1)
    (rest,) = main(add_kernel, "sum0", (rest, rest_far), [shape(later_rows + RANK // 2, LANES)])
    rest_far = pair(rest, 1, 1)
    pay, keep = main(node_kernel, "node", (rest, rest_far, cores), [shape(PAY + RANK, LANES), two], 2, 2)
    pay_far = pair(pay, 2, 1)
    near, prod = call(take_kernel, "late1", (late, late_far), [shape(LANES, LANES), shape(tail, LANES)], after=(rest,))
    near_far = pair(near, 0)
    prod_far = pair(prod, 2)
    w2, half = main(level2_kernel, "level2", (pay, pay_far), [one, one])
    half_far = pair(half, 3, 1)
    (prod,) = call(add_kernel, "late2", (prod, prod_far), [shape(tail, LANES)], after=(pay_far,))
    prod_far = pair(prod, 3)
    w23, keep = main(
        level3_kernel, "level3", (half, half_far, cores, w2, keep, near, near_far), [one, two], 3, 2, (prod,)
    )
    keep_far = pair(keep, 2, 1)
    (prod,) = call(add_core_kernel, "late3", (prod, prod_far, cores), [shape(tail + RANK, LANES)], 4, 2, (half_far,))
    prod_near, far_prod = pair(prod, 0), pair(prod, 4)
    (keep,) = main(add_kernel, "sum2", (keep, keep_far), [two], after=(prod,))
    keep_far = pair(keep, 3, 1)
    (far_copy,) = call(copy_kernel, "late4", (far_prod,), [shape(*far_prod.shape)], after=(w23,))
    (keep,) = main(add_kernel, "sum3", (keep, keep_far), [two], after=(far_copy,))
    keep_far = pair(keep, 4, 1)
    w4, keep = main(
        level4_kernel,
        "level4",
        (keep, keep_far, prod, prod_near, far_prod, pair(far_copy, 0), cores),
        [one, shape(2 * RHS + 2 * RANK + RANK // 2, LANES)],
        5,
        6,
    )
    w5, keep = main(level5_kernel, "level5", (keep, pair(keep, 5, 1), cores), [one, shape(PAY + RANK, LANES)], 6, 2)
    w6, keep = main(level6_kernel, "level6", (keep, pair(keep, 6, 1)), [one, one])
    keep_far = pair(keep, 7, 1)
    placed, basis = call(
        place_kernel,
        "place",
        (current, w01, w23, w4, w5, w6, trial, point_order),
        [shape(RHS, leaf), jax.ShapeDtypeStruct((RANK, leaf), BF16)],
        limit=32,
    )
    return call(
        last_kernel, "last", (keep, keep_far, cores, placed, basis), [shape(RHS, leaf)], level=7, at=2
    )[0]


def solution(mesh):
    in_specs = (
        P(None, "leaf"),
        P("leaf", None),
        P("leaf", None),
        P(None, None, "leaf"),
        P(None, None, "leaf"),
        P(None, "leaf", None),
    )
    out_specs = P(None, "leaf")
    return jax.shard_map(local, mesh=mesh, in_specs=in_specs, out_specs=out_specs, check_vma=False)
```

```python
import functools

import jax
import jax.numpy as jnp
from jax import lax
from jax.experimental import pallas as pl
from jax.experimental.pallas import tpu as pltpu
from jax.sharding import PartitionSpec as P


F32 = jnp.float32
BF16 = jnp.bfloat16
PAIRS = 4
RHS = 16
RANK = 64
LANES = 128
WIDE = 256
CHUNKS = 4
NT = (((1,), (1,)), ((), ()))
PAY = RHS + RANK // 2


def split(x, parts):
    out = []
    for _ in range(parts):
        piece = x.astype(BF16)
        out.append(piece)
        x = x - piece.astype(F32)
    return out


def times(weights, product):
    high, low = split(product, 2)
    return jnp.dot(weights, high, preferred_element_type=F32) + jnp.dot(weights, low, preferred_element_type=F32)


def core_times(stacked, cores):
    rows = stacked.shape[0]
    out = lax.dot_general(jnp.concatenate(split(stacked, 3), axis=0), cores, NT, preferred_element_type=F32)
    return (out[:rows] + (out[rows : 2 * rows] + out[2 * rows :])).astype(BF16)


def lanes(rows=RHS):
    return lax.broadcasted_iota(jnp.int32, (rows, LANES), 1)


def swap(x):
    return pltpu.roll(x, RANK, 1)


def bit(k):
    return lax.axis_index("leaf") >> k & 1


def order(k, own, far):
    upper = bit(k) == 1
    return jnp.where(upper, far, own), jnp.where(upper, own, far)


def shared_out(own, other):
    second = (bit(0) + bit(1) + bit(2) + bit(4)) & 1 == 1
    return jnp.where(second, other, own), jnp.where(second, own, other)


def side_by_side(k, low, high):
    if k % 2:
        return jnp.where(lanes() < RANK, swap(low), high)
    return jnp.where(lanes() < RANK, low, swap(high))


def one_hot_low(positions, leaf):
    rows = lax.broadcasted_iota(jnp.int32, (WIDE, leaf), 0)
    return jnp.where(rows == (positions & (WIDE - 1)), 1.0, 0.0).astype(BF16)


def gather_points(sides, positions):
    leaf = sides.shape[1]
    high = positions // WIDE
    rows = jnp.concatenate([sides[:, h * WIDE : (h + 1) * WIDE] for h in range(leaf // WIDE)], axis=0)
    picked = jnp.dot(rows, one_hot_low(positions, leaf), preferred_element_type=F32)
    total = jnp.zeros((RHS, leaf), F32)
    for h in range(leaf // WIDE):
        total = total + jnp.where(high == h, picked[h * RHS : (h + 1) * RHS], 0.0)
    return total.astype(BF16)


def chunked(leaf, pairs, sems):
    width = leaf // CHUNKS
    copies = []
    for j in range(CHUNKS):
        at = pl.ds(j * width, width)
        copies.append(
            [pltpu.make_async_copy(src.at[:, at], dst.at[:, at], sems.at[i, j]) for i, (src, dst) in enumerate(pairs)]
        )
        for copy in copies[-1]:
            copy.start()
    return copies


def pack(right):
    half = RANK // 2
    return jnp.where(lanes(half) < RANK, swap(right[:half]), right[half:])


def unpack(rows):
    both = jnp.concatenate([swap(rows), rows], axis=0)
    return jnp.where(lanes(RANK) < RANK, 0.0, both)


def ready_kernel(out_ref):
    out_ref[...] = jnp.zeros_like(out_ref)


def leaf_kernel(
    rs_ref, pos_ref, inv_hbm, u_hbm, v_hbm, cur_ref, pay_ref, rest_ref, near_ref, inv, u, v, ordered, both, sems
):
    leaf = rs_ref.shape[1]
    width = leaf // CHUNKS
    copies = chunked(leaf, [(inv_hbm, inv), (u_hbm, u), (v_hbm.at[:LANES], v)], sems)
    ordered[...] = gather_points(rs_ref[...], pos_ref[...])
    for j in range(CHUNKS):
        for copy in copies[j]:
            copy.wait()
        lo, hi = j * width, (j + 1) * width
        current = jnp.dot(ordered[...], inv[:, lo:hi], preferred_element_type=F32)
        cur_ref[:, lo:hi] = current
        rows = jnp.concatenate([current.astype(BF16), v[:, lo:hi]], axis=0)
        part = lax.dot_general(rows, u[:, lo:hi], NT, preferred_element_type=F32)
        if j == 0:
            both[...] = part
        else:
            both[...] += part
    pay_ref[:RHS] = both[:RHS, :LANES]
    pay_ref[RHS:] = pack(both[RHS : RHS + RANK, :LANES])
    for b in range(1, PAIRS):
        rest_ref[(b - 1) * RHS : b * RHS] = both[:RHS, b * LANES : (b + 1) * LANES]
        near_ref[(b - 1) * LANES : b * LANES] = both[RHS:, b * LANES : (b + 1) * LANES]


def products_kernel(u_hbm, v_hbm, diag_ref, keep_ref, send_ref, u, v, gram, sems):
    leaf = u.shape[1]
    width = leaf // CHUNKS
    copies = chunked(leaf, [(u_hbm.at[LANES:], u), (v_hbm.at[LANES:], v)], sems)
    for j in range(CHUNKS):
        for copy in copies[j]:
            copy.wait()
        lo, hi = j * width, (j + 1) * width
        part = lax.dot_general(v[:, lo:hi], u[:, lo:hi], NT, preferred_element_type=F32)
        if j == 0:
            gram[...] = part
        else:
            gram[...] += part

    def tile(a, b):
        return gram[(a - 1) * LANES : a * LANES, (b - 1) * LANES : b * LANES]

    diag_ref[...] = pack(tile(1, 1)[:RANK])
    diag = jnp.where(lanes(RANK) < RANK, swap(tile(2, 2)[:RANK]), tile(3, 3)[:RANK])
    tail = jnp.concatenate([tile(2, 3), diag], axis=0)
    cut = tail.shape[0] // 2
    halves = [jnp.concatenate([tile(1, 2), tail[:cut]], axis=0), jnp.concatenate([tile(1, 3), tail[cut:]], axis=0)]
    keep_ref[...], send_ref[...] = shared_out(*halves)


def first_kernel(pay_ref, core_ref, out_ref):
    rows = pay_ref.shape[0]
    out_ref[:rows] = pay_ref[...]
    out_ref[rows:] = core_ref[0].astype(F32)


def even_step(k, own_ref, far_ref, w_ref, out_ref):
    own, far = own_ref[:RHS], far_ref[:RHS]
    both = both_weights(k, own, far, own_ref[PAY:], far_ref[PAY:])
    w_ref[...] = both.astype(F32)
    at = slice(RHS, PAY)
    diag = jnp.concatenate([unpack(own_ref[at]), unpack(far_ref[at])], axis=0)
    out_ref[...] = (own + far) - times(both, diag)


def level0_kernel(own_ref, far_ref, w_ref, out_ref):
    even_step(0, own_ref, far_ref, w_ref, out_ref)


def level2_kernel(own_ref, far_ref, w_ref, out_ref):
    even_step(2, own_ref, far_ref, w_ref, out_ref)


def odd_weights(k, own_ref, far_ref, core_ref, even_ref, w_ref):
    stacked = side_by_side(k, *order(k, own_ref[...], far_ref[...]))
    w_ref[:, :RANK] = even_ref[:, :RANK]
    w_ref[:, RANK:] = core_times(stacked, core_ref[0]).astype(F32)
    return w_ref[...].astype(BF16)


def level1_kernel(own_ref, far_ref, core_ref, even_ref, rest_ref, near_ref, diag_ref, w_ref, out_ref):
    both = odd_weights(1, own_ref, far_ref, core_ref, even_ref, w_ref)
    later = PAIRS - 1
    for i in range(later):
        rows = slice(i * RHS, (i + 1) * RHS)
        out_ref[rows] = rest_ref[rows] - times(both, near_ref[i * LANES : (i + 1) * LANES])
    out_ref[later * RHS :] = diag_ref[...]


def node_kernel(own_ref, far_ref, core_ref, pay_ref, keep_ref):
    total = own_ref[...] + far_ref[...]
    later = PAIRS - 1
    pay_ref[:RHS] = total[:RHS]
    pay_ref[RHS:PAY] = total[later * RHS :]
    pay_ref[PAY:] = core_ref[0].astype(F32)
    keep_ref[...] = total[RHS : later * RHS]


def level3_kernel(own_ref, far_ref, core_ref, even_ref, keep_ref, near_ref, far_near_ref, w_ref, out_ref):
    both = odd_weights(3, own_ref, far_ref, core_ref, even_ref, w_ref)
    for i, product in enumerate(shared_out(near_ref[...], far_near_ref[...])):
        rows = slice(i * RHS, (i + 1) * RHS)
        out_ref[rows] = keep_ref[rows] - times(both, product)


def add_kernel(a_ref, b_ref, out_ref):
    out_ref[...] = a_ref[...] + b_ref[...]


def copy_kernel(a_ref, out_ref):
    out_ref[...] = a_ref[...]


def add_core_kernel(a_ref, b_ref, core_ref, out_ref):
    rows = a_ref.shape[0]
    out_ref[:rows] = a_ref[...] + b_ref[...]
    out_ref[rows:] = core_ref[0].astype(F32)


def take_kernel(a_ref, b_ref, near_ref, out_ref):
    rows = near_ref.shape[0]
    near_ref[...] = a_ref[:rows] + b_ref[:rows]
    out_ref[...] = a_ref[rows:] + b_ref[rows:]


def both_weights(k, own, far, core, far_core):
    stacked = side_by_side(k, *order(k, own, far))
    return core_times(stacked, jnp.concatenate([core, far_core], axis=0).astype(BF16))


def level4_kernel(
    own_ref, far_ref, prod_ref, prod_near_ref, far_prod_ref, far_near_ref, core_ref, w_ref, out_ref
):
    own, far = own_ref[...], far_ref[...]
    rows = prod_ref.shape[0] - RANK
    both = both_weights(4, own[:RHS], far[:RHS], prod_ref[rows:], far_prod_ref[rows:])
    w_ref[...] = both.astype(F32)
    mine = jnp.concatenate(shared_out(prod_ref[:rows], prod_near_ref[:rows]), axis=0)
    theirs = jnp.concatenate(shared_out(far_prod_ref[:rows], far_near_ref[:rows]), axis=0)
    cross = jnp.concatenate([mine[:RANK], theirs[:RANK]], axis=0)
    diag = jnp.concatenate([mine[LANES:], theirs[LANES:]], axis=0)
    diag = jnp.where(lanes(LANES) < RANK, 0.0, swap(diag))
    total = own + far
    out_ref[:RHS] = total[:RHS] - times(both, diag)
    out_ref[RHS : 2 * RHS] = total[RHS:] - times(both, cross)
    later = mine[RANK:] + theirs[RANK:]
    out_ref[2 * RHS : 2 * RHS + RANK] = later[:RANK]
    out_ref[2 * RHS + RANK : 2 * RHS + RANK + RANK // 2] = pack(later[RANK:])
    out_ref[2 * RHS + RANK + RANK // 2 :] = core_ref[0].astype(F32)


def level5_kernel(own_ref, far_ref, core_ref, w_ref, out_ref):
    cores = slice(2 * RHS + RANK + RANK // 2, own_ref.shape[0])
    both = both_weights(5, own_ref[:RHS], far_ref[:RHS], own_ref[cores], far_ref[cores])
    w_ref[...] = both.astype(F32)
    at = slice(2 * RHS, 2 * RHS + RANK)
    cross = jnp.concatenate([own_ref[at], far_ref[at]], axis=0)
    out_ref[:RHS] = (own_ref[RHS : 2 * RHS] + far_ref[RHS : 2 * RHS]) - times(both, cross)
    at = slice(2 * RHS + RANK, 2 * RHS + RANK + RANK // 2)
    out_ref[RHS:PAY] = own_ref[at] + far_ref[at]
    out_ref[PAY:] = core_ref[0].astype(F32)


def level6_kernel(own_ref, far_ref, w_ref, out_ref):
    even_step(6, own_ref, far_ref, w_ref, out_ref)


def scatter_points(values, positions):
    leaf = positions.shape[1]
    high = positions // WIDE
    count = leaf // WIDE
    parts = jnp.concatenate([x.astype(F32) for x in values], axis=0)
    rows = parts.shape[0]
    chosen = jnp.concatenate([jnp.where(high == h, parts, 0.0).astype(BF16) for h in range(count)], axis=0)
    moved = lax.dot_general(chosen, one_hot_low(positions, leaf), NT, preferred_element_type=F32)
    return [moved[h * rows : (h + 1) * rows] for h in range(count)]


def place_kernel(cur_ref, w01_ref, w23_ref, w4_ref, w5_ref, w6_ref, v_ref, pos_ref, out_ref, basis_ref):
    weights = [w01_ref[...].astype(BF16), w23_ref[...].astype(BF16)]
    weights += [w_ref[:, :RANK].astype(BF16) for w_ref in (w4_ref, w5_ref, w6_ref)]
    known = v_ref.shape[0] - RANK
    current = cur_ref[...] - jnp.dot(jnp.concatenate(weights, axis=1), v_ref[:known], preferred_element_type=F32)
    for h, block in enumerate(scatter_points(split(current, 2) + [v_ref[known:]], pos_ref[...])):
        at = slice(h * WIDE, (h + 1) * WIDE)
        out_ref[:, at] = block[:RHS] + block[RHS : 2 * RHS]
        basis_ref[:, at] = block[2 * RHS :].astype(BF16)


def last_kernel(own_ref, far_ref, core_ref, placed_ref, basis_ref, out_ref):
    weights = core_times(side_by_side(7, *order(7, own_ref[...], far_ref[...])), core_ref[0])
    out_ref[...] = placed_ref[...] - jnp.dot(weights, basis_ref[...], preferred_element_type=F32)


def local(right_sides, point_order, leaf_inverse, test_bases, trial_bases, coupling_cores):
    devices = lax.axis_size("leaf")
    leaf = right_sides.shape[1]
    total = PAIRS * LANES
    test = test_bases.reshape(total, leaf)
    trial = trial_bases.reshape(total, leaf)
    vmem = pl.BlockSpec(memory_space=pltpu.VMEM)
    anywhere = pl.BlockSpec(memory_space=pl.ANY)
    hbm = pl.BlockSpec(memory_space=pltpu.HBM)

    def shape(*dims):
        return jax.ShapeDtypeStruct(dims, F32)

    def core(level):
        return pl.BlockSpec((1, RANK, LANES), lambda *_: (level, 0, 0))

    def call(kernel, name, args, shapes, level=None, at=None, after=(), limit=16, hint=0):
        count = len(args)
        specs = [vmem] * count + [anywhere] * len(after)
        grid = {}
        if at is not None:
            specs[at] = core(level)
            grid = {"grid": (1,)}

        def body(*refs):
            kernel(*refs[:count], *refs[count + len(after) :])

        return pl.pallas_call(
            body,
            in_specs=specs,
            out_specs=[vmem] * len(shapes),
            out_shape=shapes,
            compiler_params=pltpu.CompilerParams(vmem_limit_bytes=limit * 2**20),
            name=name,
            cost_estimate=pl.CostEstimate(flops=hint, bytes_accessed=0, transcendentals=0) if hint else None,
            **grid,
        )(*args, *after)

    main = functools.partial(call, hint=int(6e9))

    def pair(values, k, across=0):
        mask = {3: 3 << 2, 5: 3 << 4, 7: 3 << 6}.get(k, 1 << k) ^ across
        return lax.ppermute(values, "leaf", [(d, d ^ mask) for d in range(devices)])

    cores = coupling_cores
    tail = (LANES + RANK) // 2
    late_rows = LANES + tail
    later_rows = (PAIRS - 1) * RHS
    big = pltpu.CompilerParams(vmem_limit_bytes=52 * 2**20)
    (ready,) = main(ready_kernel, "ready", (), [shape(8, LANES)])

    def leaf_body(after_ref, *refs):
        leaf_kernel(*refs)

    current, pay, rest, near = pl.pallas_call(
        leaf_body,
        in_specs=[anywhere, vmem, vmem, anywhere, anywhere, anywhere],
        out_specs=[vmem] * 4,
        out_shape=[
            shape(RHS, leaf),
            shape(PAY, LANES),
            shape(later_rows, LANES),
            shape((PAIRS - 1) * LANES, LANES),
        ],
        scratch_shapes=[
            pltpu.VMEM((leaf, leaf), BF16),
            pltpu.VMEM((total, leaf), BF16),
            pltpu.VMEM((LANES, leaf), BF16),
            pltpu.VMEM((RHS, leaf), BF16),
            pltpu.VMEM((RHS + LANES, total), F32),
            pltpu.SemaphoreType.DMA((3, CHUNKS)),
        ],
        compiler_params=big,
        name="leaf",
    )(ready, right_sides, point_order, leaf_inverse, test, trial)

    one = shape(RHS, LANES)
    two = shape(2 * RHS, LANES)

    (pay,) = call(first_kernel, "first", (pay, cores), [shape(PAY + RANK, LANES)], 0, 1)
    w0, half = main(level0_kernel, "level0", (pay, pair(pay, 0)), [one, one])
    half_far = pair(half, 1, 1)

    def products_body(after_ref, *refs):
        products_kernel(*refs)

    diag, late, late_send = pl.pallas_call(
        products_body,
        in_specs=[anywhere] * 3,
        out_specs=[vmem] * 3,
        out_shape=[shape(RANK // 2, LANES), shape(late_rows, LANES), shape(late_rows, LANES)],
        scratch_shapes=[
            pltpu.VMEM((total - LANES, leaf), BF16),
            pltpu.VMEM((total - LANES, leaf), BF16),
            pltpu.VMEM((total - LANES, total - LANES), F32),
            pltpu.SemaphoreType.DMA((2, CHUNKS)),
        ],
        compiler_params=big,
        cost_estimate=pl.CostEstimate(flops=2 * leaf * (total - LANES) ** 2, bytes_accessed=4 * leaf * (total - LANES), transcendentals=0),
        name="products",
    )(half, test, trial)
    late_far = pair(late_send, 0)
    w01, rest = main(
        level1_kernel,
        "level1",
        (half, half_far, cores, w0, rest, near, diag),
        [one, shape(later_rows + RANK // 2, LANES)],
        1,
        2,
    )
    rest_far = pair(rest, 0)
    (late,) = call(add_kernel, "late0", (late, late_far), [shape(late_rows, LANES)], after=(w01,))
    late_far = pair(late, 1, 1)
    (rest,) = main(add_kernel, "sum0", (rest, rest_far), [shape(later_rows + RANK // 2, LANES)])
    rest_far = pair(rest, 1, 1)
    pay, keep = main(node_kernel, "node", (rest, rest_far, cores), [shape(PAY + RANK, LANES), two], 2, 2)
    pay_far = pair(pay, 2, 1)
    near, prod = call(take_kernel, "late1", (late, late_far), [shape(LANES, LANES), shape(tail, LANES)], after=(rest,))
    near_far = pair(near, 0)
    prod_far = pair(prod, 2, 1)
    w2, half = main(level2_kernel, "level2", (pay, pay_far), [one, one])
    half_far = pair(half, 3, 1)
    (prod,) = call(add_kernel, "late2", (prod, prod_far), [shape(tail, LANES)], after=(pay_far,))
    prod_far = pair(prod, 3, 1)
    w23, keep = main(
        level3_kernel, "level3", (half, half_far, cores, w2, keep, near, near_far), [one, two], 3, 2, (prod,)
    )
    keep_far = pair(keep, 2, 1)
    (prod,) = call(add_core_kernel, "late3", (prod, prod_far, cores), [shape(tail + RANK, LANES)], 4, 2, (half_far,))
    prod_near, far_prod = pair(prod, 0), pair(prod, 4, 1)
    (keep,) = main(add_kernel, "sum2", (keep, keep_far), [two], after=(prod,))
    keep_far = pair(keep, 3, 1)
    (far_copy,) = call(copy_kernel, "late4", (far_prod,), [shape(*far_prod.shape)], after=(w23,))
    (keep,) = main(add_kernel, "sum3", (keep, keep_far), [two], after=(far_copy,))
    keep_far = pair(keep, 4, 1)
    w4, keep = main(
        level4_kernel,
        "level4",
        (keep, keep_far, prod, prod_near, far_prod, pair(far_copy, 0), cores),
        [one, shape(2 * RHS + 2 * RANK + RANK // 2, LANES)],
        5,
        6,
    )
    w5, keep = main(level5_kernel, "level5", (keep, pair(keep, 5, 1), cores), [one, shape(PAY + RANK, LANES)], 6, 2)
    w6, keep = main(level6_kernel, "level6", (keep, pair(keep, 6, 1)), [one, one])
    keep_far = pair(keep, 7, 1)
    placed, basis = call(
        place_kernel,
        "place",
        (current, w01, w23, w4, w5, w6, trial, point_order),
        [shape(RHS, leaf), jax.ShapeDtypeStruct((RANK, leaf), BF16)],
        limit=32,
    )
    return call(
        last_kernel, "last", (keep, keep_far, cores, placed, basis), [shape(RHS, leaf)], level=7, at=2
    )[0]


def solution(mesh):
    in_specs = (
        P(None, "leaf"),
        P("leaf", None),
        P("leaf", None),
        P(None, None, "leaf"),
        P(None, None, "leaf"),
        P(None, "leaf", None),
    )
    out_specs = P(None, "leaf")
    return jax.shard_map(local, mesh=mesh, in_specs=in_specs, out_specs=out_specs, check_vma=False)
```

```python
import functools

import jax
import jax.numpy as jnp
from jax import lax
from jax.experimental import pallas as pl
from jax.experimental.pallas import tpu as pltpu
from jax.sharding import PartitionSpec as P


F32 = jnp.float32
BF16 = jnp.bfloat16
PAIRS = 4
RHS = 16
RANK = 64
LANES = 128
WIDE = 256
CHUNKS = 4
NT = (((1,), (1,)), ((), ()))
PAY = RHS + RANK // 2


def split(x, parts):
    out = []
    for _ in range(parts):
        piece = x.astype(BF16)
        out.append(piece)
        x = x - piece.astype(F32)
    return out


def times(weights, product):
    return jnp.dot(
        jnp.concatenate([weights, weights], axis=1),
        jnp.concatenate(split(product, 2), axis=0),
        preferred_element_type=F32,
    )


def core_times(stacked, cores):
    rows = stacked.shape[0]
    out = lax.dot_general(jnp.concatenate(split(stacked, 2), axis=0), cores, NT, preferred_element_type=F32)
    return (out[:rows] + out[rows:]).astype(BF16)


def lanes(rows=RHS):
    return lax.broadcasted_iota(jnp.int32, (rows, LANES), 1)


def swap(x):
    return pltpu.roll(x, RANK, 1)


def bit(k):
    return lax.axis_index("leaf") >> k & 1


def order(k, own, far):
    upper = bit(k) == 1
    return jnp.where(upper, far, own), jnp.where(upper, own, far)


def shared_out(own, other):
    second = (bit(0) + bit(1) + bit(2) + bit(4)) & 1 == 1
    return jnp.where(second, other, own), jnp.where(second, own, other)


def side_by_side(k, low, high):
    if k % 2:
        return jnp.where(lanes() < RANK, swap(low), high)
    return jnp.where(lanes() < RANK, low, swap(high))


def one_hot_low(positions, leaf):
    rows = lax.broadcasted_iota(jnp.int32, (WIDE, leaf), 0)
    return jnp.where(rows == (positions & (WIDE - 1)), 1.0, 0.0).astype(BF16)


def gather_points(sides, positions):
    leaf = sides.shape[1]
    high = positions // WIDE
    rows = jnp.concatenate([sides[:, h * WIDE : (h + 1) * WIDE] for h in range(leaf // WIDE)], axis=0)
    picked = jnp.dot(rows, one_hot_low(positions, leaf), preferred_element_type=F32)
    total = jnp.zeros((RHS, leaf), F32)
    for h in range(leaf // WIDE):
        total = total + jnp.where(high == h, picked[h * RHS : (h + 1) * RHS], 0.0)
    return total.astype(BF16)


def chunked(leaf, pairs, sems):
    width = leaf // CHUNKS
    copies = []
    for j in range(CHUNKS):
        at = pl.ds(j * width, width)
        copies.append(
            [pltpu.make_async_copy(src.at[:, at], dst.at[:, at], sems.at[i, j]) for i, (src, dst) in enumerate(pairs)]
        )
        for copy in copies[-1]:
            copy.start()
    return copies


def pack(right):
    half = RANK // 2
    return jnp.where(lanes(half) < RANK, swap(right[:half]), right[half:])


def unpack(rows):
    both = jnp.concatenate([swap(rows), rows], axis=0)
    return jnp.where(lanes(RANK) < RANK, 0.0, both)


def ready_kernel(out_ref):
    out_ref[...] = jnp.zeros_like(out_ref)


def leaf_kernel(
    rs_ref, pos_ref, inv_hbm, u_hbm, v_hbm, cur_ref, pay_ref, rest_ref, near_ref, inv, u, v, ordered, both, sems
):
    leaf = rs_ref.shape[1]
    width = leaf // CHUNKS
    copies = chunked(leaf, [(inv_hbm, inv), (u_hbm, u), (v_hbm.at[:LANES], v)], sems)
    ordered[...] = gather_points(rs_ref[...], pos_ref[...])
    for j in range(CHUNKS):
        for copy in copies[j]:
            copy.wait()
        lo, hi = j * width, (j + 1) * width
        current = jnp.dot(ordered[...], inv[:, lo:hi], preferred_element_type=F32)
        cur_ref[:, lo:hi] = current
        rows = jnp.concatenate([current.astype(BF16), v[:, lo:hi]], axis=0)
        part = lax.dot_general(rows, u[:, lo:hi], NT, preferred_element_type=F32)
        if j == 0:
            both[...] = part
        else:
            both[...] += part
    pay_ref[:RHS] = both[:RHS, :LANES]
    pay_ref[RHS:] = pack(both[RHS : RHS + RANK, :LANES])
    for b in range(1, PAIRS):
        rest_ref[(b - 1) * RHS : b * RHS] = both[:RHS, b * LANES : (b + 1) * LANES]
        near_ref[(b - 1) * LANES : b * LANES] = both[RHS:, b * LANES : (b + 1) * LANES]


def products_kernel(u_hbm, v_hbm, diag_ref, keep_ref, send_ref, u, v, gram, sems):
    leaf = u.shape[1]
    width = leaf // CHUNKS
    copies = chunked(leaf, [(u_hbm.at[LANES:], u), (v_hbm.at[LANES:], v)], sems)
    for j in range(CHUNKS):
        for copy in copies[j]:
            copy.wait()
        lo, hi = j * width, (j + 1) * width
        part = lax.dot_general(v[:, lo:hi], u[:, lo:hi], NT, preferred_element_type=F32)
        if j == 0:
            gram[...] = part
        else:
            gram[...] += part

    def tile(a, b):
        return gram[(a - 1) * LANES : a * LANES, (b - 1) * LANES : b * LANES]

    diag_ref[...] = pack(tile(1, 1)[:RANK])
    diag = jnp.where(lanes(RANK) < RANK, swap(tile(2, 2)[:RANK]), tile(3, 3)[:RANK])
    tail = jnp.concatenate([tile(2, 3), diag], axis=0)
    cut = tail.shape[0] // 2
    halves = [jnp.concatenate([tile(1, 2), tail[:cut]], axis=0), jnp.concatenate([tile(1, 3), tail[cut:]], axis=0)]
    keep_ref[...], send_ref[...] = shared_out(*halves)


def first_kernel(pay_ref, core_ref, out_ref):
    rows = pay_ref.shape[0]
    out_ref[:rows] = pay_ref[...]
    out_ref[rows:] = core_ref[0].astype(F32)


def even_step(k, own_ref, far_ref, w_ref, out_ref):
    own, far = own_ref[:RHS], far_ref[:RHS]
    both = both_weights(k, own, far, own_ref[PAY:], far_ref[PAY:])
    w_ref[...] = both.astype(F32)
    at = slice(RHS, PAY)
    diag = jnp.concatenate([unpack(own_ref[at]), unpack(far_ref[at])], axis=0)
    out_ref[...] = (own + far) - times(both, diag)


def level0_kernel(own_ref, far_ref, w_ref, out_ref):
    even_step(0, own_ref, far_ref, w_ref, out_ref)


def level2_kernel(own_ref, far_ref, w_ref, out_ref):
    even_step(2, own_ref, far_ref, w_ref, out_ref)


def odd_weights(k, own_ref, far_ref, core_ref, even_ref, w_ref):
    stacked = side_by_side(k, *order(k, own_ref[...], far_ref[...]))
    w_ref[:, :RANK] = even_ref[:, :RANK]
    w_ref[:, RANK:] = core_times(stacked, core_ref[0]).astype(F32)
    return w_ref[...].astype(BF16)


def level1_kernel(own_ref, far_ref, core_ref, even_ref, rest_ref, near_ref, diag_ref, w_ref, out_ref):
    both = odd_weights(1, own_ref, far_ref, core_ref, even_ref, w_ref)
    later = PAIRS - 1
    for i in range(later):
        rows = slice(i * RHS, (i + 1) * RHS)
        out_ref[rows] = rest_ref[rows] - times(both, near_ref[i * LANES : (i + 1) * LANES])
    out_ref[later * RHS :] = diag_ref[...]


def node_kernel(own_ref, far_ref, core_ref, pay_ref, keep_ref):
    total = own_ref[...] + far_ref[...]
    later = PAIRS - 1
    pay_ref[:RHS] = total[:RHS]
    pay_ref[RHS:PAY] = total[later * RHS :]
    pay_ref[PAY:] = core_ref[0].astype(F32)
    keep_ref[...] = total[RHS : later * RHS]


def level3_kernel(own_ref, far_ref, core_ref, even_ref, keep_ref, near_ref, far_near_ref, w_ref, out_ref):
    both = odd_weights(3, own_ref, far_ref, core_ref, even_ref, w_ref)
    for i, product in enumerate(shared_out(near_ref[...], far_near_ref[...])):
        rows = slice(i * RHS, (i + 1) * RHS)
        out_ref[rows] = keep_ref[rows] - times(both, product)


def add_kernel(a_ref, b_ref, out_ref):
    out_ref[...] = a_ref[...] + b_ref[...]


def copy_kernel(a_ref, out_ref):
    out_ref[...] = a_ref[...]


def add_core_kernel(a_ref, b_ref, core_ref, out_ref):
    rows = a_ref.shape[0]
    out_ref[:rows] = a_ref[...] + b_ref[...]
    out_ref[rows:] = core_ref[0].astype(F32)


def take_kernel(a_ref, b_ref, near_ref, out_ref):
    rows = near_ref.shape[0]
    near_ref[...] = a_ref[:rows] + b_ref[:rows]
    out_ref[...] = a_ref[rows:] + b_ref[rows:]


def both_weights(k, own, far, core, far_core):
    stacked = side_by_side(k, *order(k, own, far))
    return core_times(stacked, jnp.concatenate([core, far_core], axis=0).astype(BF16))


def level4_kernel(
    own_ref, far_ref, prod_ref, prod_near_ref, far_prod_ref, far_near_ref, core_ref, w_ref, out_ref
):
    own, far = own_ref[...], far_ref[...]
    rows = prod_ref.shape[0] - RANK
    both = both_weights(4, own[:RHS], far[:RHS], prod_ref[rows:], far_prod_ref[rows:])
    w_ref[...] = both.astype(F32)
    mine = jnp.concatenate(shared_out(prod_ref[:rows], prod_near_ref[:rows]), axis=0)
    theirs = jnp.concatenate(shared_out(far_prod_ref[:rows], far_near_ref[:rows]), axis=0)
    cross = jnp.concatenate([mine[:RANK], theirs[:RANK]], axis=0)
    diag = jnp.concatenate([mine[LANES:], theirs[LANES:]], axis=0)
    diag = jnp.where(lanes(LANES) < RANK, 0.0, swap(diag))
    total = own + far
    out_ref[:RHS] = total[:RHS] - times(both, diag)
    out_ref[RHS : 2 * RHS] = total[RHS:] - times(both, cross)
    later = mine[RANK:] + theirs[RANK:]
    out_ref[2 * RHS : 2 * RHS + RANK] = later[:RANK]
    out_ref[2 * RHS + RANK : 2 * RHS + RANK + RANK // 2] = pack(later[RANK:])
    out_ref[2 * RHS + RANK + RANK // 2 :] = core_ref[0].astype(F32)


def level5_kernel(own_ref, far_ref, core_ref, w_ref, out_ref):
    cores = slice(2 * RHS + RANK + RANK // 2, own_ref.shape[0])
    both = both_weights(5, own_ref[:RHS], far_ref[:RHS], own_ref[cores], far_ref[cores])
    w_ref[...] = both.astype(F32)
    at = slice(2 * RHS, 2 * RHS + RANK)
    cross = jnp.concatenate([own_ref[at], far_ref[at]], axis=0)
    out_ref[:RHS] = (own_ref[RHS : 2 * RHS] + far_ref[RHS : 2 * RHS]) - times(both, cross)
    at = slice(2 * RHS + RANK, 2 * RHS + RANK + RANK // 2)
    out_ref[RHS:PAY] = own_ref[at] + far_ref[at]
    out_ref[PAY:] = core_ref[0].astype(F32)


def level6_kernel(own_ref, far_ref, w_ref, out_ref):
    even_step(6, own_ref, far_ref, w_ref, out_ref)


def scatter_points(values, positions):
    leaf = positions.shape[1]
    high = positions // WIDE
    count = leaf // WIDE
    parts = jnp.concatenate([x.astype(F32) for x in values], axis=0)
    rows = parts.shape[0]
    chosen = jnp.concatenate([jnp.where(high == h, parts, 0.0).astype(BF16) for h in range(count)], axis=0)
    moved = lax.dot_general(chosen, one_hot_low(positions, leaf), NT, preferred_element_type=F32)
    return [moved[h * rows : (h + 1) * rows] for h in range(count)]


def place_kernel(cur_ref, w01_ref, w23_ref, w4_ref, w5_ref, w6_ref, v_ref, pos_ref, out_ref, basis_ref):
    weights = [w01_ref[...].astype(BF16), w23_ref[...].astype(BF16)]
    weights += [w_ref[:, :RANK].astype(BF16) for w_ref in (w4_ref, w5_ref, w6_ref)]
    known = v_ref.shape[0] - RANK
    current = cur_ref[...] - jnp.dot(jnp.concatenate(weights, axis=1), v_ref[:known], preferred_element_type=F32)
    for h, block in enumerate(scatter_points(split(current, 2) + [v_ref[known:]], pos_ref[...])):
        at = slice(h * WIDE, (h + 1) * WIDE)
        out_ref[:, at] = block[:RHS] + block[RHS : 2 * RHS]
        basis_ref[:, at] = block[2 * RHS :].astype(BF16)


def last_kernel(own_ref, far_ref, core_ref, placed_ref, basis_ref, out_ref):
    weights = core_times(side_by_side(7, *order(7, own_ref[...], far_ref[...])), core_ref[0])
    out_ref[...] = placed_ref[...] - jnp.dot(weights, basis_ref[...], preferred_element_type=F32)


def local(right_sides, point_order, leaf_inverse, test_bases, trial_bases, coupling_cores):
    devices = lax.axis_size("leaf")
    leaf = right_sides.shape[1]
    total = PAIRS * LANES
    test = test_bases.reshape(total, leaf)
    trial = trial_bases.reshape(total, leaf)
    vmem = pl.BlockSpec(memory_space=pltpu.VMEM)
    anywhere = pl.BlockSpec(memory_space=pl.ANY)
    hbm = pl.BlockSpec(memory_space=pltpu.HBM)

    def shape(*dims):
        return jax.ShapeDtypeStruct(dims, F32)

    def core(level):
        return pl.BlockSpec((1, RANK, LANES), lambda *_: (level, 0, 0))

    def call(kernel, name, args, shapes, level=None, at=None, after=(), limit=16, hint=0):
        count = len(args)
        specs = [vmem] * count + [anywhere] * len(after)
        grid = {}
        if at is not None:
            specs[at] = core(level)
            grid = {"grid": (1,)}

        def body(*refs):
            kernel(*refs[:count], *refs[count + len(after) :])

        return pl.pallas_call(
            body,
            in_specs=specs,
            out_specs=[vmem] * len(shapes),
            out_shape=shapes,
            compiler_params=pltpu.CompilerParams(vmem_limit_bytes=limit * 2**20),
            name=name,
            cost_estimate=pl.CostEstimate(flops=hint, bytes_accessed=0, transcendentals=0) if hint else None,
            **grid,
        )(*args, *after)

    main = functools.partial(call, hint=int(6e9))

    def pair(values, k, across=0):
        mask = {3: 3 << 2, 5: 3 << 4, 7: 3 << 6}.get(k, 1 << k) ^ across
        return lax.ppermute(values, "leaf", [(d, d ^ mask) for d in range(devices)])

    cores = coupling_cores
    tail = (LANES + RANK) // 2
    late_rows = LANES + tail
    later_rows = (PAIRS - 1) * RHS
    big = pltpu.CompilerParams(vmem_limit_bytes=52 * 2**20)
    (ready,) = main(ready_kernel, "ready", (), [shape(8, LANES)])

    def leaf_body(after_ref, *refs):
        leaf_kernel(*refs)

    current, pay, rest, near = pl.pallas_call(
        leaf_body,
        in_specs=[anywhere, vmem, vmem, anywhere, anywhere, anywhere],
        out_specs=[vmem] * 4,
        out_shape=[
            shape(RHS, leaf),
            shape(PAY, LANES),
            shape(later_rows, LANES),
            shape((PAIRS - 1) * LANES, LANES),
        ],
        scratch_shapes=[
            pltpu.VMEM((leaf, leaf), BF16),
            pltpu.VMEM((total, leaf), BF16),
            pltpu.VMEM((LANES, leaf), BF16),
            pltpu.VMEM((RHS, leaf), BF16),
            pltpu.VMEM((RHS + LANES, total), F32),
            pltpu.SemaphoreType.DMA((3, CHUNKS)),
        ],
        compiler_params=big,
        name="leaf",
    )(ready, right_sides, point_order, leaf_inverse, test, trial)

    one = shape(RHS, LANES)
    two = shape(2 * RHS, LANES)

    (pay,) = call(first_kernel, "first", (pay, cores), [shape(PAY + RANK, LANES)], 0, 1)
    w0, half = main(level0_kernel, "level0", (pay, pair(pay, 0)), [one, one])
    half_far = pair(half, 1, 1)

    def products_body(after_ref, *refs):
        products_kernel(*refs)

    diag, late, late_send = pl.pallas_call(
        products_body,
        in_specs=[anywhere] * 3,
        out_specs=[vmem] * 3,
        out_shape=[shape(RANK // 2, LANES), shape(late_rows, LANES), shape(late_rows, LANES)],
        scratch_shapes=[
            pltpu.VMEM((total - LANES, leaf), BF16),
            pltpu.VMEM((total - LANES, leaf), BF16),
            pltpu.VMEM((total - LANES, total - LANES), F32),
            pltpu.SemaphoreType.DMA((2, CHUNKS)),
        ],
        compiler_params=big,
        cost_estimate=pl.CostEstimate(flops=2 * leaf * (total - LANES) ** 2, bytes_accessed=4 * leaf * (total - LANES), transcendentals=0),
        name="products",
    )(half, test, trial)
    late_far = pair(late_send, 0)
    w01, rest = main(
        level1_kernel,
        "level1",
        (half, half_far, cores, w0, rest, near, diag),
        [one, shape(later_rows + RANK // 2, LANES)],
        1,
        2,
    )
    rest_far = pair(rest, 0)
    (late,) = call(add_kernel, "late0", (late, late_far), [shape(late_rows, LANES)], after=(w01,))
    late_far = pair(late, 1, 1)
    (rest,) = main(add_kernel, "sum0", (rest, rest_far), [shape(later_rows + RANK // 2, LANES)])
    rest_far = pair(rest, 1, 1)
    pay, keep = main(node_kernel, "node", (rest, rest_far, cores), [shape(PAY + RANK, LANES), two], 2, 2)
    pay_far = pair(pay, 2, 1)
    near, prod = call(take_kernel, "late1", (late, late_far), [shape(LANES, LANES), shape(tail, LANES)], after=(rest,))
    near_far = pair(near, 0)
    prod_far = pair(prod, 2, 1)
    w2, half = main(level2_kernel, "level2", (pay, pay_far), [one, one])
    half_far = pair(half, 3, 1)
    (prod,) = call(add_kernel, "late2", (prod, prod_far), [shape(tail, LANES)], after=(pay_far,))
    prod_far = pair(prod, 3, 1)
    w23, keep = main(
        level3_kernel, "level3", (half, half_far, cores, w2, keep, near, near_far), [one, two], 3, 2, (prod,)
    )
    keep_far = pair(keep, 2, 1)
    (prod,) = call(add_core_kernel, "late3", (prod, prod_far, cores), [shape(tail + RANK, LANES)], 4, 2, (half_far,))
    prod_near, far_prod = pair(prod, 0), pair(prod, 4, 1)
    (keep,) = main(add_kernel, "sum2", (keep, keep_far), [two], after=(prod,))
    keep_far = pair(keep, 3, 1)
    (far_copy,) = call(copy_kernel, "late4", (far_prod,), [shape(*far_prod.shape)], after=(w23,))
    (keep,) = main(add_kernel, "sum3", (keep, keep_far), [two], after=(far_copy,))
    keep_far = pair(keep, 4, 1)
    w4, keep = main(
        level4_kernel,
        "level4",
        (keep, keep_far, prod, prod_near, far_prod, pair(far_copy, 0), cores),
        [one, shape(2 * RHS + 2 * RANK + RANK // 2, LANES)],
        5,
        6,
    )
    w5, keep = main(level5_kernel, "level5", (keep, pair(keep, 5, 1), cores), [one, shape(PAY + RANK, LANES)], 6, 2)
    w6, keep = main(level6_kernel, "level6", (keep, pair(keep, 6, 1)), [one, one])
    keep_far = pair(keep, 7, 1)
    placed, basis = call(
        place_kernel,
        "place",
        (current, w01, w23, w4, w5, w6, trial, point_order),
        [shape(RHS, leaf), jax.ShapeDtypeStruct((RANK, leaf), BF16)],
        limit=32,
    )
    return call(
        last_kernel, "last", (keep, keep_far, cores, placed, basis), [shape(RHS, leaf)], level=7, at=2
    )[0]


def solution(mesh):
    in_specs = (
        P(None, "leaf"),
        P("leaf", None),
        P("leaf", None),
        P(None, None, "leaf"),
        P(None, None, "leaf"),
        P(None, "leaf", None),
    )
    out_specs = P(None, "leaf")
    return jax.shard_map(local, mesh=mesh, in_specs=in_specs, out_specs=out_specs, check_vma=False)
```
